512 devices in a mesh: gx: 32 (over z, core), gy: 16 (over x, y).
Axes of the slice: x: 4, y: 4, z: 16, core: 2. Of those that a mesh axis runs over, the one named last changes fastest.
Arguments:
- offsets: float32 [6144, 3, 128], P(('gx', 'gy')), may hold values from 0 to 1
- widths: float32 [6144, 128], P(('gx', 'gy')), may hold values from 0.6 to 2.5
- solvation: float32 [6144, 128], P(('gx', 'gy')), may hold values from -6 to 6
- heading: int32 [6144, 1], P(('gx', 'gy')), may hold values from 0 to 8; in each aligned block of 12 rows (0 to 11, 12 to 23, ...) at most 3 rows name the same one
- old_map: float32 [256, 384, 1024], P('gx', 'gy'), may hold values from -6 to 6
Outputs:
- new_map: float32 [256, 384, 1024], P('gx', 'gy')
The draws below stay inside these ranges and needn't reach their ends.
Inputs may be any that keep to these rules, and one draw needn't show every extreme that they name: `heading`: entry d moves a block d // 3 - 1 tiles along x and d % 3 - 1 tiles along y from the tile of the device that stores it; among the 12 blocks of one device at most 3 share an entry.
All inputs are finite; a program needn't handle non-finite values.
Results may differ from the reference program's by a relative error of at most 0.0003.
Values sent between devices are 32-bit elements; how exact they have to be, the bound alone decides.
No kernel may reach another device: no remote copies, remote signals or barrier semaphores. Data moves between devices by JAX's collectives and lax.ppermute only.
A program may use at most 64 MiB of HBM per device.

```python
import math
import jax
import jax.numpy as jnp
import numpy as np
from jax import lax

TX = 8
TY = 24
NZ = 1024
B_DEV = 12
ATOM_BLOCK = 128
SLOTS = 3
W = 5
NX = 256
NY = 384
NBLK = 6144
N_GX = 32
N_GY = 16


def level_of(rng, dims, cuts, least, largest):
    def one(position, parts):
        draws = jax.random.uniform(jax.random.fold_in(jax.random.fold_in(rng, 6), position), (parts,), jnp.float32, least / len(cuts), largest / len(cuts))
        return jnp.repeat(jnp.exp(draws), dims[position] // parts).reshape((-1,) + (1,) * (len(dims) - position - 1))

    gain = one(*cuts[0])
    for cut in cuts[1:]:
        gain = gain * one(*cut)
    return gain


def shared_out(rng, own, number, rows, number_of, top, most, lean):
    ranking = jax.random.permutation(rng, number_of)
    heavy_load, usual = portions_of(number_of, rows * top, most, lean, True), portions_of(number_of, rows * top, most, lean, False)
    places = jnp.arange(number_of)

    def named(lengths, rotation):
        used = int((lengths > 0).sum())
        fixed = max(1, used // 4)
        passed = fixed + (places - fixed + rotation * (used - fixed)) % max(1, number_of - fixed)
        return jnp.zeros((number_of,), jnp.int32).at[ranking[jnp.where(places < fixed, places, passed)]].set(jnp.asarray(lengths, jnp.int32))

    lengths = jnp.where(number % 4 == 0, named(heavy_load, number // 4), named(usual, number - number // 4 - 1))
    mixed = jax.random.permutation(jax.random.fold_in(own, 3), number_of)
    donor, sink = mixed[0:number_of // 2 * 2:2], mixed[1:number_of // 2 * 2:2]
    margin = jnp.minimum(lengths[donor] - 1, most - lengths[sink]) // 2
    margin = jnp.where((donor == ranking[0]) | (sink == ranking[0]) | (lengths[sink] == 0), 0, jnp.maximum(margin, 0))
    passed = jax.random.randint(jax.random.fold_in(own, 4), (number_of // 2,), 0, 1 << 20) % (margin + 1)
    lengths = lengths.at[donor].add(-passed).at[sink].add(passed)
    members = jnp.searchsorted(jnp.cumsum(lengths), jnp.arange(rows * top), side="right").astype(jnp.int32)
    listing = members.reshape(top, rows).T
    listing = listing[jax.random.permutation(jax.random.fold_in(own, 1), rows)]
    rotation = jax.random.randint(jax.random.fold_in(own, 2), (rows, 1), 0, top)
    return jnp.take_along_axis(listing, (jnp.arange(top)[None, :] + rotation) % top, axis=1)


def portions_of(count, total, bound, skew, full):
    loads = [(1 << 20) // math.isqrt(rank ** skew) + 1 for rank in range(1, count + 1)]
    largest = bound if full else min(bound, max(-(-total // count), total * loads[0] // sum(loads)))
    least = 1 if total - largest >= count - 1 else 0
    given, rest = [largest] + [least] * (count - 1), total - largest - least * (count - 1)
    while rest > 0:
        movable = [i for i in range(1, count) if given[i] < largest] or [i for i in range(1, count) if given[i] < bound]
        pool, budget = sum([loads[i] for i in movable]), rest
        for i in movable:
            addition = min(bound - given[i], max(1, budget * loads[i] // pool), rest)
            given[i] = given[i] + addition
            rest = rest - addition
    return np.array(given)


def gaussian(stream_key, dims, spread, bound, split=(), held_as=jnp.bfloat16):
    gain = level_of(stream_key, dims, split, -0.22, 0.18) if split else 1.0
    values = jax.random.normal(stream_key, dims, jnp.float32) * spread * gain
    return jnp.minimum(jnp.maximum(values, -bound), bound).astype(held_as)


def setup_inputs(seed: int = 0) -> dict:
    seeds = jax.random.split(jax.random.key(seed), 6)
    offsets = jnp.clip(1.0 * jax.random.uniform(seeds[0], (NBLK, 3, ATOM_BLOCK), jnp.float32) ** level_of(seeds[0], (NBLK, 3, ATOM_BLOCK), ((0, 512),), -0.2, 0.2), 0.0, 1.0)
    widths = jnp.clip(jnp.exp(math.log(2.5) - 1.4271163 * jax.random.uniform(seeds[1], (NBLK, ATOM_BLOCK), jnp.float32) ** level_of(seeds[1], (NBLK, ATOM_BLOCK), ((0, 512),), -0.2, 0.2)), 0.6, 2.5)
    solvation = gaussian(seeds[2], (NBLK, ATOM_BLOCK), 1.0, 6.0, ((0, 512),), jnp.float32)
    heading_keys = jax.random.split(jax.random.fold_in(seeds[3], 1), NBLK // B_DEV)
    heading_turns = jax.random.permutation(jax.random.fold_in(seeds[3], 3), NBLK // B_DEV)
    heading = jax.vmap(lambda own, number: shared_out(jax.random.fold_in(seeds[3], 2), own, number, B_DEV, 9, 1, SLOTS, 2))(heading_keys, heading_turns).reshape((NBLK, 1))
    old_map = gaussian(seeds[4], (NX, NY, NZ), 1.0, 6.0, ((0, 32), (1, 16)), jnp.float32)
    return dict(offsets=offsets, widths=widths, solvation=solvation, heading=heading, old_map=old_map)


def block_field(rel, width_row, weight_row, span_x, span_y, span_z):
    alpha = 0.5 / (width_row * width_row)
    delta_x = span_x[None, :] - rel[0][:, None]
    delta_y = span_y[None, :] - rel[1][:, None]
    delta_z = span_z[None, :] - rel[2][:, None]
    along_x = jnp.exp(-alpha[:, None] * delta_x * delta_x)
    along_y = jnp.exp(-alpha[:, None] * delta_y * delta_y)
    along_z = jnp.exp(-alpha[:, None] * delta_z * delta_z)
    plane = weight_row[:, None, None] * along_x[:, :, None] * along_y[:, None, :]
    plane = plane.reshape(plane.shape[0], -1)
    return lax.dot_general(plane, along_z, (((0,), (0,)), ((), ())), precision=lax.Precision.HIGHEST)


def reference(offsets, widths, solvation, heading, old_map):
    ext_x = TX + 2 * W
    ext_y = TY + 2 * W
    span_x = jnp.arange(ext_x).astype(jnp.float32) - W
    span_y = jnp.arange(ext_y).astype(jnp.float32) - W
    span_z = jnp.arange(NZ).astype(jnp.float32)
    grid = jnp.zeros((NX + 2 * W, NY + 2 * W, NZ), jnp.float32)
    count = offsets.shape[0]

    def step(total, inputs):
        place, width_row, weight_row, target, number = inputs
        device = number // B_DEV
        tile_row = device // N_GY + target // 3 - 1
        tile_col = device % N_GY + target % 3 - 1
        inside = (tile_row >= 0) & (tile_row < N_GX) & (tile_col >= 0) & (tile_col < N_GY)
        weight_row = jnp.where(inside, weight_row, jnp.zeros_like(weight_row))
        rel = (place[0] * TX, place[1] * TY, place[2] * NZ)
        field = block_field(rel, width_row, weight_row, span_x, span_y, span_z).reshape(ext_x, ext_y, NZ)
        start_x = (jnp.clip(tile_row, 0, N_GX - 1) * TX).astype(jnp.int32)
        start_y = (jnp.clip(tile_col, 0, N_GY - 1) * TY).astype(jnp.int32)
        start_z = jnp.zeros((), jnp.int32)
        window = lax.dynamic_slice(total, (start_x, start_y, start_z), (ext_x, ext_y, NZ))
        total = lax.dynamic_update_slice(total, window + field, (start_x, start_y, start_z))
        return total, None

    numbers = jnp.arange(count).astype(jnp.int32)
    grid, unused = lax.scan(step, grid, (offsets, widths, solvation, heading[:, 0], numbers))
    return old_map + grid[W:W + NX, W:W + NY, :]
```

```python
import functools
import jax
import jax.numpy as jnp
from jax import lax
from jax.experimental import pallas as pl
from jax.experimental.pallas import tpu as pltpu
from jax.sharding import PartitionSpec as P

LOG2E = 1.4426950408889634
NT = (((1,), (1,)), ((), ()))
FAR = 1.0e6
f32 = jnp.float32
ROWS = (192, 272, 192)
START = (0, 192, 464)

def quotient(n, d):
    shift = 16
    return lax.shift_right_logical(n * (((1 << shift) + d - 1) // d), shift)

def fill_tables(ti, tj):
    for g in range(3):
        n = ROWS[g]
        m = lax.broadcasted_iota(jnp.int32, (n, 128), 0)
        if g == 1:
            core, e = m < 192, m - 192
            right = e >= 40
            e = jnp.where(right, e - 40, e)
            ci = quotient(m, 24)
            dead = None
        else:
            core, e = m < 120, m - 120
            right = e >= 32
            e = jnp.where(right, e - 32, e)
            dead = e >= 32
            ci = quotient(m, 24)
            if g == 2:
                e = e + 8
        cj = m - ci * 24
        if g == 2:
            ci = ci + 3
        e = jnp.maximum(e, 0)
        ei = quotient(e, 5)
        ej = e - ei * 5 + jnp.where(right, 24, -5)
        i = jnp.where(core, ci, ei)
        j = jnp.where(core, cj, ej)
        i = (i + (8, 0, -8)[g]).astype(f32)
        if dead is not None:
            out = (ei >= 5) if g == 0 else (ei < 3)
            i = jnp.where((~core) & (out | dead), FAR, i)
        ti[START[g]:START[g] + n, :] = i
        tj[START[g]:START[g] + n, :] = j.astype(f32)

def split(v):
    h = v.astype(jnp.bfloat16)
    return h, (v - h.astype(f32)).astype(jnp.bfloat16)

def field_kernel(own_ref, p1_ref, p2_ref, m1_ref, m2_ref, old_ref, core_ref, left_ref, right_ref,
                 lists, acc, ti, tj):
    depth = old_ref.shape[2]
    fill_tables(ti, tj)
    acc[...] = jnp.zeros_like(acc)
    sources = (
        ((own_ref, 0), (p1_ref, 0), (p2_ref, 0)),
        ((own_ref, 1), (p1_ref, 1), (m1_ref, 0)),
        ((own_ref, 2), (m1_ref, 1), (m2_ref, 0)),
    )
    row = lax.broadcasted_iota(jnp.int32, (8, 128), 0)
    dead = jnp.where(row == 3, 1.0, 0.0).astype(f32)
    counts = []
    for g in range(3):
        cnt = jnp.int32(0)
        for ref, part in sources[g]:
            seg = ref[part]
            bits = jnp.zeros((1, 128), f32)
            for s in range(9):
                bits = bits + seg[s, 5:6, :] * float(1 << s)
            mask = jnp.max(bits).astype(jnp.int32)
            for s in range(9):
                lists[g, cnt] = seg[s]
                cnt = cnt + (lax.shift_right_logical(mask, s) & 1)
        lists[g, cnt] = dead
        counts.append(cnt)
    kio = lax.broadcasted_iota(jnp.int32, (256, 1), 0).astype(f32)

    def pair(g, p):
        n = ROWS[g]
        rec = jnp.concatenate([lists[g, 2 * p], lists[g, 2 * p + 1]], axis=1)
        x, y, z = rec[0:1] * 8.0, rec[1:2] * 24.0, rec[2:3] * 1024.0
        c = (-0.5 * LOG2E) / (rec[3:4] * rec[3:4])
        weight = rec[4:5]
        tic = ti[START[g]:START[g] + n, :]
        tjc = tj[START[g]:START[g] + n, :]
        dx = jnp.concatenate([tic, tic], axis=1) - x
        dy = jnp.concatenate([tjc, tjc], axis=1) - y
        ph, plo = split(jnp.exp2((dx * dx + dy * dy) * c) * weight)
        for b in range(depth // 256):
            ks = slice(b * 256, b * 256 + 256)
            d = kio + (b * 256.0 - z)
            zh, zl = split(jnp.exp2(d * (d * c)))
            dot = functools.partial(lax.dot_general, dimension_numbers=NT, preferred_element_type=f32)
            t = dot(jnp.concatenate([ph, plo], 0), zh)
            r = t[:n] + t[n:] + dot(ph, zl)
            if g == 1:
                acc[:, ks] += r
            elif g == 0:
                acc[0:120, ks] += r[0:120]
                acc[192:224, ks] += r[120:152]
                acc[232:264, ks] += r[152:184]
            else:
                acc[72:192, ks] += r[0:120]
                acc[200:232, ks] += r[120:152]
                acc[240:272, ks] += r[152:184]

    for g in range(3):
        def step(p, carry, g=g):
            pair(g, p)
            return carry
        lax.fori_loop(0, lax.shift_right_logical(counts[g] + 1, 1), step, 0)
    core_ref[...] = old_ref[...] + acc[0:192, :].reshape(core_ref.shape)
    left_ref[...] = acc[192:232, :]
    right_ref[...] = acc[232:272, :]


def pack_kernel(heading, offsets, widths, solvation, minus, same, plus, slots, taken):
    slots[...] = jnp.zeros_like(slots)
    for h in range(9):
        taken[h] = 0
    tile_row, tile_rows = lax.axis_index("gx"), lax.axis_size("gx")
    for b in range(offsets.shape[0]):
        h = heading[b, 0]
        n = taken[h]
        taken[h] = n + 1
        row, col = lax.div(h, 3), lax.rem(h, 3)
        place = col * 9 + row * 3 + n
        slots[place, 0:3, :] = offsets[b]
        slots[place, 3:4, :] = widths[b:b + 1, :]
        slots[place, 4:5, :] = solvation[b:b + 1, :]
        home = tile_row + row - 1
        inside = (home >= 0) & (home < tile_rows)
        slots[place, 5:6, :] = jnp.full((1, 128), jnp.where(inside, 1.0, 0.0), f32)
    for k, out in enumerate((minus, same, plus)):
        out[...] = slots[9 * k:9 * k + 9].reshape(out.shape)


def edge_kernel(core, from_left, from_right, out):
    side = pl.program_id(0)
    out[...] = core[...]

    @pl.when(side == 0)
    def _():
        for i in range(8):
            out[i, 0:5, :] += from_left[i * 5:i * 5 + 5, :]

    @pl.when(side == 1)
    def _():
        for i in range(8):
            out[i, 3:8, :] += from_right[i * 5:i * 5 + 5, :]


def passed_along(value, axis, steps):
    count = lax.axis_size(axis)
    first, last = (max(0, -steps), min(count, count - steps))
    return lax.ppermute(value, axis, [(source, source + steps) for source in range(first, last)])


def body(offsets, widths, solvation, heading, old_map):
    depth = old_map.shape[2]
    vm = pl.BlockSpec(memory_space=pltpu.VMEM)
    third = jax.ShapeDtypeStruct((3, 3, 8, 128), f32)
    minus, same, plus = pl.pallas_call(
        pack_kernel,
        out_shape=[third] * 3,
        in_specs=[pl.BlockSpec(memory_space=pltpu.SMEM), vm, vm, vm],
        out_specs=[vm] * 3,
        scratch_shapes=[pltpu.VMEM((27, 8, 128), f32), pltpu.SMEM((9,), jnp.int32)],
        name="pack",
    )(heading, offsets, widths, solvation)
    own = jnp.concatenate(
        [same, passed_along(plus, "gy", 1), passed_along(minus, "gy", -1)], axis=1
    )
    above1 = passed_along(own[1:3], "gx", 1)
    above2 = passed_along(own[2:3], "gx", 2)
    below1 = passed_along(own[0:2], "gx", -1)
    below2 = passed_along(own[0:1], "gx", -2)
    edge = jax.ShapeDtypeStruct((40, depth), f32)
    core, left, right = pl.pallas_call(
        field_kernel,
        out_shape=[jax.ShapeDtypeStruct(old_map.shape, f32), edge, edge],
        in_specs=[vm] * 6,
        out_specs=[vm] * 3,
        scratch_shapes=[
            pltpu.VMEM((3, 28, 8, 128), f32),
            pltpu.VMEM((272, depth), f32),
            pltpu.VMEM((656, 128), f32),
            pltpu.VMEM((656, 128), f32),
        ],
        compiler_params=pltpu.CompilerParams(vmem_limit_bytes=40 * 1024 * 1024),
        name="field",
    )(own, above1, above2, below1, below2, old_map)
    from_left = passed_along(right, "gy", 1)
    from_right = passed_along(left, "gy", -1)
    block = pl.BlockSpec((8, 8, depth), lambda s: (0, 2 * s, 0))
    whole = pl.BlockSpec((40, depth), lambda s: (0, 0))
    return pl.pallas_call(
        edge_kernel,
        grid=(2,),
        out_shape=jax.ShapeDtypeStruct(old_map.shape, f32),
        in_specs=[block, whole, whole],
        out_specs=block,
        input_output_aliases={0: 0},
        name="edges",
    )(core, from_left, from_right)


def solution(mesh):
    placed = (
        P(("gx", "gy"), None, None),
        P(("gx", "gy"), None),
        P(("gx", "gy"), None),
        P(("gx", "gy"), None),
        P("gx", "gy", None),
    )
    return jax.shard_map(
        body, mesh=mesh, in_specs=placed, out_specs=P("gx", "gy", None), check_vma=False
    )
```

```python
import functools
import jax
import jax.numpy as jnp
from jax import lax
from jax.experimental import pallas as pl
from jax.experimental.pallas import tpu as pltpu
from jax.sharding import PartitionSpec as P

LOG2E = 1.4426950408889634
FAR = 1.0e6
W = 5
f32, bf16 = jnp.float32, jnp.bfloat16
ABOVE, OWN, BELOW = 0, 1, 2
CORE_ROWS = (128, 192, 128)
EDGE_ROWS = (64, 80, 64)


def quotient(n, d):
    return lax.shift_right_logical(n * ((65536 + d - 1) // d), 16)


def put_rows(ti, tj, start, group, core):
    n = (CORE_ROWS if core else EDGE_ROWS)[group]
    m = lax.broadcasted_iota(jnp.int32, (n, 128), 0)
    if core:
        row = m + (64 if group == BELOW else 0)
        i = quotient(row, 24)
        j = row - i * 24
    else:
        side = m >= n // 2
        e = jnp.where(side, m - n // 2, m) + (8 if group == BELOW else 0)
        i = quotient(e, 5)
        j = e - i * 5 + jnp.where(side, 24, -W)
    place = (i + (8, 0, -8)[group]).astype(f32)
    if group == ABOVE:
        place = jnp.where(i >= W, FAR, place)
    if group == BELOW:
        place = jnp.where(i < 8 - W, FAR, place)
    ti[start:start + n, :] = place
    tj[start:start + n, :] = j.astype(f32)


def split(v):
    h = v.astype(bf16)
    return h, (v - h.astype(f32)).astype(bf16)


def compact(lists, group, sources, blocks):
    row = lax.broadcasted_iota(jnp.int32, (8, 128), 0)
    dead = jnp.where(row == 3, 1.0, 0.0).astype(f32)
    count = jnp.int32(0)
    for ref, part in sources:
        bits = jnp.zeros((1, 128), f32)
        for s in range(9):
            bits = bits + ref[part, s, 5:6, :] * float(1 << s)
        mask = jnp.max(bits).astype(jnp.int32)
        for s in range(9):
            lists[group, count] = ref[part, s]
            count = count + (lax.shift_right_logical(mask, s) & 1)
    for s in range(blocks - 1):
        lists[group, count + s] = dead
    return lax.div(count + (blocks - 1), jnp.int32(blocks))


def add_field(lists, steps, ti, tj, rows, starts, adds, depth, blocks, wide):
    k_io = lax.broadcasted_iota(jnp.int32, (1, wide), 1).astype(f32)
    dot = functools.partial(jnp.dot, preferred_element_type=f32)

    def stage(g, t):
        n = rows[g]
        recs = [lists[g, t * blocks + q] for q in range(blocks)]
        rec = jnp.concatenate(recs, axis=1)
        x, y, weight = rec[0:1] * 8.0, rec[1:2] * 24.0, rec[4:5]
        c = (-0.5 * LOG2E) / (rec[3:4] * rec[3:4])
        ri, rj = ti[starts[g]:starts[g] + n, :], tj[starts[g]:starts[g] + n, :]
        dx = jnp.concatenate([ri] * blocks, axis=1) - x
        dy = jnp.concatenate([rj] * blocks, axis=1) - y
        ph, plo = split(jnp.exp2((dx * dx + dy * dy) * c) * weight)
        cols = jnp.concatenate([jnp.transpose(r) for r in recs], axis=0)
        z = cols[:, 2:3] * 1024.0
        cz = (-0.5 * LOG2E) / (cols[:, 3:4] * cols[:, 3:4])

        def along(b):
            d = k_io - (z - float(b * wide))
            return split(jnp.exp2(d * (d * cz)))

        nxt = along(0)
        for b in range(depth // wide):
            zh, zl = nxt
            if b + 1 < depth // wide:
                nxt = along(b + 1)
            r = dot(jnp.concatenate([ph, plo, ph], 1), jnp.concatenate([zh, zh, zl], 0))
            for ref, to, count, source in adds[g]:
                ref[to:to + count, b * wide:(b + 1) * wide] += r[source:source + count]

    for g in range(3):
        def step(t, carry, g=g):
            stage(g, t)
            return carry
        lax.fori_loop(0, steps[g], step, 0)


def core_adds(ref):
    return [[(ref, 0, 128, 0)], [(ref, 0, 192, 0)], [(ref, 64, 128, 0)]]


def edge_adds(left, right):
    return [
        [(left, 0, 32, 0), (right, 0, 32, 32)],
        [(left, 0, 40, 0), (right, 0, 40, 40)],
        [(left, 8, 32, 0), (right, 8, 32, 32)],
    ]


def both_adds(core, left, right):
    return [
        a + [(ref, to, n, source + CORE_ROWS[g]) for ref, to, n, source in b]
        for g, (a, b) in enumerate(zip(core_adds(core), edge_adds(left, right)))
    ]


def prepare(ti, tj, kinds):
    rows, starts, at = [], [], 0
    for g in range(3):
        starts.append(at)
        for core in kinds:
            put_rows(ti, tj, at, g, core)
            at += (CORE_ROWS if core else EDGE_ROWS)[g]
        rows.append(at - starts[-1])
    return rows, starts


BLOCKS, WIDE = 4, 256


def first_kernel(own, old, core, left, right, lists, ti, tj):
    depth = core.shape[1]
    rows, starts = prepare(ti, tj, (True, False))
    core[...] = old[...].reshape(core.shape)
    for ref in (left, right):
        ref[...] = jnp.zeros_like(ref)
    steps = [compact(lists, g, ((own, g),), BLOCKS) for g in range(3)]
    add_field(lists, steps, ti, tj, rows, starts, both_adds(core, left, right), depth, BLOCKS, WIDE)


def others(above, below, beside):
    return (
        ((above, 1), (beside, 0)),
        ((beside, 1), (beside, 2)),
        ((below, 0), (beside, 3)),
    )


def rest_kernel(above, below, beside, core0, left0, right0, core, left, right, lists, ti, tj):
    depth = core.shape[1]
    rows, starts = prepare(ti, tj, (True, False))
    core[...] = core0[...]
    left[...] = left0[...]
    right[...] = right0[...]
    steps = [compact(lists, g, s, BLOCKS) for g, s in enumerate(others(above, below, beside))]
    add_field(lists, steps, ti, tj, rows, starts, both_adds(core, left, right), depth, BLOCKS, WIDE)


VM = pl.BlockSpec(memory_space=pltpu.VMEM)


def call(kernel, name, outs, rows, capacity, cost, *operands):
    return pl.pallas_call(
        kernel,
        out_shape=[jax.ShapeDtypeStruct(s, f32) for s in outs],
        in_specs=[VM] * len(operands),
        out_specs=[VM] * len(outs),
        scratch_shapes=[
            pltpu.VMEM((3, capacity, 8, 128), f32),
            pltpu.VMEM((rows, 128), f32),
            pltpu.VMEM((rows, 128), f32),
        ],
        compiler_params=pltpu.CompilerParams(vmem_limit_bytes=32 * 1024 * 1024),
        cost_estimate=pl.CostEstimate(
            flops=int(cost * 2e8), bytes_accessed=4_000_000, transcendentals=int(cost * 300_000)
        ),
        name=name,
    )(*operands)


def pack_kernel(heading, offsets, widths, solvation, minus, same, plus, slots, taken):
    slots[...] = jnp.zeros_like(slots)
    for h in range(9):
        taken[h] = 0
    tile_row, tile_rows = lax.axis_index("gx"), lax.axis_size("gx")
    for b in range(offsets.shape[0]):
        h = heading[b]
        n = taken[h]
        taken[h] = n + 1
        row, col = lax.div(h, 3), lax.rem(h, 3)
        place = col * 9 + row * 3 + n
        slots[place, 0:3, :] = offsets[b]
        slots[place, 3:4, :] = widths[b:b + 1, :]
        slots[place, 4:5, :] = solvation[b:b + 1, :]
        home = tile_row + row - 1
        inside = (home >= 0) & (home < tile_rows)
        slots[place, 5:6, :] = jnp.full((1, 128), jnp.where(inside, 1.0, 0.0), f32)
    for k, out in enumerate((minus, same, plus)):
        out[...] = slots[9 * k:9 * k + 9].reshape(out.shape)


def edge_kernel(core, from_left, from_right, out):
    out[:, 8:16, :] = core[:, 8:16, :]
    for i in range(core.shape[0]):
        out[i, 0:8, :] = core[i, 0:8, :]
        out[i, 0:5, :] += from_left[i * 5:i * 5 + 5, :]
        out[i, 16:24, :] = core[i, 16:24, :]
        out[i, 19:24, :] += from_right[i * 5:i * 5 + 5, :]


def passed_along(value, axis, steps):
    count = lax.axis_size(axis)
    first, last = (max(0, -steps), min(count, count - steps))
    return lax.ppermute(value, axis, [(source, source + steps) for source in range(first, last)])


def body(offsets, widths, solvation, heading, old_map):
    depth = old_map.shape[2]
    third = jax.ShapeDtypeStruct((3, 3, 8, 128), f32)
    small = pltpu.CompilerParams(vmem_limit_bytes=8 * 1024 * 1024)
    minus, same, plus = pl.pallas_call(
        pack_kernel,
        out_shape=[third] * 3,
        in_specs=[pl.BlockSpec(memory_space=pltpu.SMEM), VM, VM, VM],
        out_specs=[VM] * 3,
        scratch_shapes=[pltpu.VMEM((27, 8, 128), f32), pltpu.SMEM((9,), jnp.int32)],
        compiler_params=small,
        name="pack",
    )(heading[:, 0], offsets, widths, solvation)
    own = jnp.concatenate(
        [same, passed_along(plus, "gy", 1), passed_along(minus, "gy", -1)], axis=1
    )
    above = passed_along(own[1:3], "gx", 2)
    below = passed_along(own[0:2], "gx", -2)
    plane, edge = (old_map.shape[0] * old_map.shape[1], depth), (40, depth)
    outs = [plane, edge, edge]
    part = call(first_kernel, "first", outs, 656, 36, 12, own, old_map)
    above, below, *part = lax.optimization_barrier((above, below, *part))
    first = lax.rem(lax.axis_index("gx"), 2) == 0
    handed = jnp.stack(
        [
            jnp.where(first, own[1], above[0]),
            jnp.where(first, own[2], own[0]),
            jnp.where(first, below[0], above[1]),
            jnp.where(first, below[1], own[1]),
        ]
    )
    pairs = [(r, r + 1 - 2 * (r % 2)) for r in range(lax.axis_size("gx"))]
    beside = lax.ppermute(handed, "gx", pairs)
    core, left, right = call(rest_kernel, "rest", outs, 656, 36, 24, above, below, beside, *part)
    from_left = passed_along(right, "gy", 1)
    from_right = passed_along(left, "gy", -1)
    return pl.pallas_call(
        edge_kernel,
        out_shape=jax.ShapeDtypeStruct(old_map.shape, f32),
        in_specs=[VM] * 3,
        out_specs=VM,
        compiler_params=small,
        name="edges",
    )(core.reshape(old_map.shape), from_left, from_right)


def solution(mesh):
    placed = (
        P(("gx", "gy"), None, None),
        P(("gx", "gy"), None),
        P(("gx", "gy"), None),
        P(("gx", "gy"), None),
        P("gx", "gy", None),
    )
    return jax.shard_map(
        body, mesh=mesh, in_specs=placed, out_specs=P("gx", "gy", None), check_vma=False
    )
```

```python
import functools
import jax
import jax.numpy as jnp
from jax import lax
from jax.experimental import pallas as pl
from jax.experimental.pallas import tpu as pltpu
from jax.sharding import PartitionSpec as P

LOG2E = 1.4426950408889634
FAR = 1.0e6
W = 5
f32, bf16 = jnp.float32, jnp.bfloat16
ABOVE, OWN, BELOW = 0, 1, 2
CORE_ROWS = (128, 192, 128)
EDGE_ROWS = (64, 80, 64)


def quotient(n, d):
    return lax.shift_right_logical(n * ((65536 + d - 1) // d), 16)


def put_rows(ti, tj, start, group, core):
    n = (CORE_ROWS if core else EDGE_ROWS)[group]
    m = lax.broadcasted_iota(jnp.int32, (n, 128), 0)
    if core:
        row = m + (64 if group == BELOW else 0)
        i = quotient(row, 24)
        j = row - i * 24
    else:
        side = m >= n // 2
        e = jnp.where(side, m - n // 2, m) + (8 if group == BELOW else 0)
        i = quotient(e, 5)
        j = e - i * 5 + jnp.where(side, 24, -W)
    place = (i + (8, 0, -8)[group]).astype(f32)
    if group == ABOVE:
        place = jnp.where(i >= W, FAR, place)
    if group == BELOW:
        place = jnp.where(i < 8 - W, FAR, place)
    ti[start:start + n, :] = place
    tj[start:start + n, :] = j.astype(f32)


def split(v):
    h = v.astype(bf16)
    return h, (v - h.astype(f32)).astype(bf16)


def compact(lists, group, sources, blocks):
    row = lax.broadcasted_iota(jnp.int32, (8, 128), 0)
    dead = jnp.where(row == 3, 1.0, 0.0).astype(f32)
    count = jnp.int32(0)
    for ref, part in sources:
        bits = jnp.zeros((1, 128), f32)
        for s in range(9):
            bits = bits + ref[part, s, 5:6, :] * float(1 << s)
        mask = jnp.max(bits).astype(jnp.int32)
        for s in range(9):
            lists[group, count] = ref[part, s]
            count = count + (lax.shift_right_logical(mask, s) & 1)
    for s in range(blocks - 1):
        lists[group, count + s] = dead
    return count


def add_field(lists, counts, ti, tj, rows, starts, adds, depth, blocks, wide):
    k_io = lax.broadcasted_iota(jnp.int32, (1, wide), 1).astype(f32)
    dot = functools.partial(jnp.dot, preferred_element_type=f32)

    def stage(g, at, blocks):
        n = rows[g]
        recs = [lists[g, at + q] for q in range(blocks)]
        rec = jnp.concatenate(recs, axis=1)
        x, y, weight = rec[0:1] * 8.0, rec[1:2] * 24.0, rec[4:5]
        c = (-0.5 * LOG2E) / (rec[3:4] * rec[3:4])
        ri, rj = ti[starts[g]:starts[g] + n, :], tj[starts[g]:starts[g] + n, :]
        dx = jnp.concatenate([ri] * blocks, axis=1) - x
        dy = jnp.concatenate([rj] * blocks, axis=1) - y
        ph, plo = split(jnp.exp2((dx * dx + dy * dy) * c) * weight)
        cols = jnp.concatenate([jnp.transpose(r) for r in recs], axis=0)
        z = cols[:, 2:3] * 1024.0
        cz = (-0.5 * LOG2E) / (cols[:, 3:4] * cols[:, 3:4])

        def along(b):
            d = k_io - (z - float(b * wide))
            return split(jnp.exp2(d * (d * cz)))

        nxt = along(0)
        for b in range(depth // wide):
            zh, zl = nxt
            if b + 1 < depth // wide:
                nxt = along(b + 1)
            r = dot(jnp.concatenate([ph, plo, ph], 1), jnp.concatenate([zh, zh, zl], 0))
            for ref, to, count, source in adds[g]:
                ref[to:to + count, b * wide:(b + 1) * wide] += r[source:source + count]

    for g in range(3):
        def step(t, carry, g=g):
            stage(g, t * blocks, blocks)
            return carry
        whole = lax.div(counts[g] + (blocks // 2 - 1), jnp.int32(blocks))
        lax.fori_loop(0, whole, step, 0)

        @pl.when(whole * blocks < counts[g])
        def _(g=g, whole=whole):
            stage(g, whole * blocks, blocks // 2)


def core_adds(ref):
    return [[(ref, 0, 128, 0)], [(ref, 0, 192, 0)], [(ref, 64, 128, 0)]]


def edge_adds(left, right):
    return [
        [(left, 0, 32, 0), (right, 0, 32, 32)],
        [(left, 0, 40, 0), (right, 0, 40, 40)],
        [(left, 8, 32, 0), (right, 8, 32, 32)],
    ]


def both_adds(core, left, right):
    return [
        a + [(ref, to, n, source + CORE_ROWS[g]) for ref, to, n, source in b]
        for g, (a, b) in enumerate(zip(core_adds(core), edge_adds(left, right)))
    ]


def prepare(ti, tj, kinds):
    rows, starts, at = [], [], 0
    for g in range(3):
        starts.append(at)
        for core in kinds:
            put_rows(ti, tj, at, g, core)
            at += (CORE_ROWS if core else EDGE_ROWS)[g]
        rows.append(at - starts[-1])
    return rows, starts


BLOCKS, WIDE = 4, 256


def first_kernel(own, core, left, right, lists, ti, tj):
    depth = core.shape[1]
    rows, starts = prepare(ti, tj, (True, False))
    for ref in (core, left, right):
        ref[...] = jnp.zeros_like(ref)
    counts = [compact(lists, g, ((own, g),), BLOCKS) for g in range(3)]
    add_field(lists, counts, ti, tj, rows, starts, both_adds(core, left, right), depth, BLOCKS, WIDE)


def others(above, below, beside):
    return (
        ((above, 1), (beside, 0)),
        ((beside, 1), (beside, 2)),
        ((below, 0), (beside, 3)),
    )


def rest_kernel(above, below, beside, core0, left0, right0, core, left, right, lists, ti, tj):
    depth = core.shape[1]
    rows, starts = prepare(ti, tj, (True, False))
    core[...] = core0[...]
    left[...] = left0[...]
    right[...] = right0[...]
    counts = [compact(lists, g, s, BLOCKS) for g, s in enumerate(others(above, below, beside))]
    add_field(lists, counts, ti, tj, rows, starts, both_adds(core, left, right), depth, BLOCKS, WIDE)


VM = pl.BlockSpec(memory_space=pltpu.VMEM)
HBM = pl.BlockSpec(memory_space=pltpu.HBM)


def call(kernel, name, outs, rows, capacity, cost, *operands):
    return pl.pallas_call(
        kernel,
        out_shape=[jax.ShapeDtypeStruct(s, f32) for s in outs],
        in_specs=[VM] * len(operands),
        out_specs=[VM] * len(outs),
        scratch_shapes=[
            pltpu.VMEM((3, capacity, 8, 128), f32),
            pltpu.VMEM((rows, 128), f32),
            pltpu.VMEM((rows, 128), f32),
        ],
        compiler_params=pltpu.CompilerParams(vmem_limit_bytes=32 * 1024 * 1024),
        cost_estimate=pl.CostEstimate(
            flops=int(cost * 2e8), bytes_accessed=4_000_000, transcendentals=int(cost * 300_000)
        ),
        name=name,
    )(*operands)


def pack_kernel(*refs):
    hbm, (minus, same, plus), local, (slots, taken, sems) = refs[:4], refs[4:7], refs[7:11], refs[11:]
    fetches = [pltpu.make_async_copy(a, b, sems.at[n]) for n, (a, b) in enumerate(zip(hbm, local))]
    for fetch in fetches:
        fetch.start()
    heading, offsets, widths, solvation = local
    slots[...] = jnp.zeros_like(slots)
    for h in range(9):
        taken[h] = 0
    for fetch in fetches:
        fetch.wait()
    tile_row, tile_rows = lax.axis_index("gx"), lax.axis_size("gx")
    for b in range(offsets.shape[0]):
        h = heading[b]
        n = taken[h]
        taken[h] = n + 1
        row, col = lax.div(h, 3), lax.rem(h, 3)
        place = col * 9 + row * 3 + n
        slots[place, 0:3, :] = offsets[b]
        slots[place, 3:4, :] = widths[b:b + 1, :]
        slots[place, 4:5, :] = solvation[b:b + 1, :]
        home = tile_row + row - 1
        inside = (home >= 0) & (home < tile_rows)
        slots[place, 5:6, :] = jnp.full((1, 128), jnp.where(inside, 1.0, 0.0), f32)
    for k, out in enumerate((minus, same, plus)):
        out[...] = slots[9 * k:9 * k + 9].reshape(out.shape)


def edge_kernel(core, old, from_left, from_right, out):
    out[...] = core[...] + old[...]
    for i in range(core.shape[0]):
        out[i, 0:5, :] += from_left[i * 5:i * 5 + 5, :]
        out[i, 19:24, :] += from_right[i * 5:i * 5 + 5, :]


def passed_along(value, axis, steps):
    count = lax.axis_size(axis)
    first, last = (max(0, -steps), min(count, count - steps))
    return lax.ppermute(value, axis, [(source, source + steps) for source in range(first, last)])


def body(offsets, widths, solvation, heading, old_map):
    depth = old_map.shape[2]
    third = jax.ShapeDtypeStruct((3, 3, 8, 128), f32)
    small = pltpu.CompilerParams(vmem_limit_bytes=8 * 1024 * 1024)
    minus, same, plus = pl.pallas_call(
        pack_kernel,
        out_shape=[third] * 3,
        in_specs=[HBM] * 4,
        out_specs=[VM] * 3,
        scratch_shapes=[
            pltpu.SMEM((offsets.shape[0],), jnp.int32),
            pltpu.VMEM(offsets.shape, f32),
            pltpu.VMEM(widths.shape, f32),
            pltpu.VMEM(solvation.shape, f32),
            pltpu.VMEM((27, 8, 128), f32),
            pltpu.SMEM((9,), jnp.int32),
            pltpu.SemaphoreType.DMA((4,)),
        ],
        compiler_params=small,
        name="pack",
    )(heading[:, 0], offsets, widths, solvation)
    own = jnp.concatenate(
        [same, passed_along(plus, "gy", 1), passed_along(minus, "gy", -1)], axis=1
    )
    above = passed_along(own[1:3], "gx", 2)
    below = passed_along(own[0:2], "gx", -2)
    plane, edge = (old_map.shape[0] * old_map.shape[1], depth), (40, depth)
    outs = [plane, edge, edge]
    part = call(first_kernel, "first", outs, 656, 36, 12, own)
    above, below, *part = lax.optimization_barrier((above, below, *part))
    first = lax.rem(lax.axis_index("gx"), 2) == 0
    handed = jnp.stack(
        [
            jnp.where(first, own[1], above[0]),
            jnp.where(first, own[2], own[0]),
            jnp.where(first, below[0], above[1]),
            jnp.where(first, below[1], own[1]),
        ]
    )
    pairs = [(r, r + 1 - 2 * (r % 2)) for r in range(lax.axis_size("gx"))]
    beside = lax.ppermute(handed, "gx", pairs)
    core, left, right = call(rest_kernel, "rest", outs, 656, 36, 24, above, below, beside, *part)
    from_left = passed_along(right, "gy", 1)
    from_right = passed_along(left, "gy", -1)
    return pl.pallas_call(
        edge_kernel,
        out_shape=jax.ShapeDtypeStruct(old_map.shape, f32),
        in_specs=[VM] * 4,
        out_specs=VM,
        compiler_params=small,
        name="edges",
    )(core.reshape(old_map.shape), old_map, from_left, from_right)


def solution(mesh):
    placed = (
        P(("gx", "gy"), None, None),
        P(("gx", "gy"), None),
        P(("gx", "gy"), None),
        P(("gx", "gy"), None),
        P("gx", "gy", None),
    )
    return jax.shard_map(
        body, mesh=mesh, in_specs=placed, out_specs=P("gx", "gy", None), check_vma=False
    )
```

```python
import functools
import jax
import jax.numpy as jnp
from jax import lax
from jax.experimental import pallas as pl
from jax.experimental.pallas import tpu as pltpu
from jax.sharding import PartitionSpec as P

LOG2E = 1.4426950408889634
FAR = 1.0e6
W = 5
f32, bf16 = jnp.float32, jnp.bfloat16
ABOVE, OWN, BELOW = 0, 1, 2
CORE_ROWS = (128, 192, 128)
EDGE_ROWS = (64, 80, 64)


def quotient(n, d):
    return lax.shift_right_logical(n * ((65536 + d - 1) // d), 16)


def put_rows(ti, tj, start, group, core):
    n = (CORE_ROWS if core else EDGE_ROWS)[group]
    m = lax.broadcasted_iota(jnp.int32, (n, 128), 0)
    if core:
        row = m + (64 if group == BELOW else 0)
        i = quotient(row, 24)
        j = row - i * 24
    else:
        side = m >= n // 2
        e = jnp.where(side, m - n // 2, m) + (8 if group == BELOW else 0)
        i = quotient(e, 5)
        j = e - i * 5 + jnp.where(side, 24, -W)
    place = (i + (8, 0, -8)[group]).astype(f32)
    if group == ABOVE:
        place = jnp.where(i >= W, FAR, place)
    if group == BELOW:
        place = jnp.where(i < 8 - W, FAR, place)
    ti[start:start + n, :] = place
    tj[start:start + n, :] = j.astype(f32)


def split(v):
    h = v.astype(bf16)
    return h, (v - h.astype(f32)).astype(bf16)


def compact(lists, group, sources, blocks):
    row = lax.broadcasted_iota(jnp.int32, (8, 128), 0)
    dead = jnp.where(row == 3, 1.0, 0.0).astype(f32)
    count = jnp.int32(0)
    for ref, part in sources:
        bits = jnp.zeros((1, 128), f32)
        for s in range(ref.shape[1]):
            bits = bits + ref[part, s, 5:6, :] * float(1 << s)
        mask = jnp.max(bits).astype(jnp.int32)
        for s in range(ref.shape[1]):
            lists[group, count] = ref[part, s]
            count = count + (lax.shift_right_logical(mask, s) & 1)
    for s in range(blocks - 1):
        lists[group, count + s] = dead
    return count


def add_field(lists, counts, ti, tj, rows, starts, adds, depth, blocks, wide):
    k_io = lax.broadcasted_iota(jnp.int32, (1, wide), 1).astype(f32)
    dot = functools.partial(jnp.dot, preferred_element_type=f32)

    def stage(g, at, blocks):
        n = rows[g]
        recs = [lists[g, at + q] for q in range(blocks)]
        rec = jnp.concatenate(recs, axis=1)
        x, y, weight = rec[0:1] * 8.0, rec[1:2] * 24.0, rec[4:5]
        c = (-0.5 * LOG2E) / (rec[3:4] * rec[3:4])
        ri, rj = ti[starts[g]:starts[g] + n, :], tj[starts[g]:starts[g] + n, :]
        dx = jnp.concatenate([ri] * blocks, axis=1) - x
        dy = jnp.concatenate([rj] * blocks, axis=1) - y
        ph, plo = split(jnp.exp2((dx * dx + dy * dy) * c) * weight)
        cols = jnp.concatenate([jnp.transpose(r) for r in recs], axis=0)
        z = cols[:, 2:3] * 1024.0
        cz = (-0.5 * LOG2E) / (cols[:, 3:4] * cols[:, 3:4])

        def along(b):
            d = k_io - (z - float(b * wide))
            return split(jnp.exp2(d * (d * cz)))

        nxt = along(0)
        for b in range(depth // wide):
            zh, zl = nxt
            if b + 1 < depth // wide:
                nxt = along(b + 1)
            r = dot(jnp.concatenate([ph, plo, ph], 1), jnp.concatenate([zh, zh, zl], 0))
            for ref, to, count, source in adds[g]:
                ref[to:to + count, b * wide:(b + 1) * wide] += r[source:source + count]

    for g in range(3):
        def step(t, carry, g=g):
            stage(g, t * blocks, blocks)
            return carry
        whole = lax.div(counts[g] + (blocks // 2 - 1), jnp.int32(blocks))
        lax.fori_loop(0, whole, step, 0)

        @pl.when(whole * blocks < counts[g])
        def _(g=g, whole=whole):
            stage(g, whole * blocks, blocks // 2)


def core_adds(ref):
    return [[(ref, 0, 128, 0)], [(ref, 0, 192, 0)], [(ref, 64, 128, 0)]]


def edge_adds(left, right):
    return [
        [(left, 0, 32, 0), (right, 0, 32, 32)],
        [(left, 0, 40, 0), (right, 0, 40, 40)],
        [(left, 8, 32, 0), (right, 8, 32, 32)],
    ]


def both_adds(core, left, right):
    return [
        a + [(ref, to, n, source + CORE_ROWS[g]) for ref, to, n, source in b]
        for g, (a, b) in enumerate(zip(core_adds(core), edge_adds(left, right)))
    ]


def prepare(ti, tj, kinds):
    rows, starts, at = [], [], 0
    for g in range(3):
        starts.append(at)
        for core in kinds:
            put_rows(ti, tj, at, g, core)
            at += (CORE_ROWS if core else EDGE_ROWS)[g]
        rows.append(at - starts[-1])
    return rows, starts


BLOCKS, WIDE = 4, 256


def field_kernel(sources, begun, *refs):
    core, left, right, lists, ti, tj = refs[-6:]
    inputs = refs[:-6]
    depth = core.shape[1]
    rows, starts = prepare(ti, tj, (True, False))
    for n, ref in enumerate((core, left, right)):
        ref[...] = inputs[len(inputs) - 3 + n][...] if begun else jnp.zeros_like(ref)
    counts = [
        compact(lists, g, [(inputs[n], part) for n, part in sources[g]], BLOCKS) for g in range(3)
    ]
    add_field(lists, counts, ti, tj, rows, starts, both_adds(core, left, right), depth, BLOCKS, WIDE)


VM = pl.BlockSpec(memory_space=pltpu.VMEM)
HBM = pl.BlockSpec(memory_space=pltpu.HBM)


def field(name, depth, blocks, sources, arrays, begun=()):
    operands = (*arrays, *begun)
    shapes = ((192, depth), (40, depth), (40, depth))
    rows = sum(CORE_ROWS) + sum(EDGE_ROWS)
    return pl.pallas_call(
        functools.partial(field_kernel, sources, bool(begun)),
        out_shape=[jax.ShapeDtypeStruct(s, f32) for s in shapes],
        in_specs=[VM] * len(operands),
        out_specs=[VM] * 3,
        scratch_shapes=[
            pltpu.VMEM((3, 27 + 2 * BLOCKS, 8, 128), f32),
            pltpu.VMEM((rows, 128), f32),
            pltpu.VMEM((rows, 128), f32),
        ],
        compiler_params=pltpu.CompilerParams(vmem_limit_bytes=32 * 1024 * 1024),
        cost_estimate=pl.CostEstimate(
            flops=blocks * 200_000_000, bytes_accessed=4_000_000, transcendentals=blocks * 300_000
        ),
        name=name,
    )(*operands)


def pack_kernel(*refs):
    hbm, (minus, same, plus), local, (slots, taken, sems) = refs[:4], refs[4:7], refs[7:11], refs[11:]
    fetches = [pltpu.make_async_copy(a, b, sems.at[n]) for n, (a, b) in enumerate(zip(hbm, local))]
    for fetch in fetches:
        fetch.start()
    heading, offsets, widths, solvation = local
    slots[...] = jnp.zeros_like(slots)
    for h in range(9):
        taken[h] = 0
    for fetch in fetches:
        fetch.wait()
    tile_row, tile_rows = lax.axis_index("gx"), lax.axis_size("gx")
    for b in range(offsets.shape[0]):
        h = heading[b]
        n = taken[h]
        taken[h] = n + 1
        row, col = lax.div(h, 3), lax.rem(h, 3)
        place = col * 9 + row * 3 + n
        slots[place, 0:3, :] = offsets[b]
        slots[place, 3:4, :] = widths[b:b + 1, :]
        slots[place, 4:5, :] = solvation[b:b + 1, :]
        home = tile_row + row - 1
        inside = (home >= 0) & (home < tile_rows)
        slots[place, 5:6, :] = jnp.full((1, 128), jnp.where(inside, 1.0, 0.0), f32)
    for k, out in enumerate((minus, same, plus)):
        out[...] = slots[9 * k:9 * k + 9].reshape(out.shape)


def edge_kernel(core, old, from_left, from_right, out):
    out[...] = core[...] + old[...]
    for i in range(core.shape[0]):
        out[i, 0:5, :] += from_left[i * 5:i * 5 + 5, :]
        out[i, 19:24, :] += from_right[i * 5:i * 5 + 5, :]


def passed_along(value, axis, steps):
    count = lax.axis_size(axis)
    first, last = (max(0, -steps), min(count, count - steps))
    return lax.ppermute(value, axis, [(source, source + steps) for source in range(first, last)])


def body(offsets, widths, solvation, heading, old_map):
    depth = old_map.shape[2]
    third = jax.ShapeDtypeStruct((3, 3, 8, 128), f32)
    small = pltpu.CompilerParams(vmem_limit_bytes=8 * 1024 * 1024)
    minus, same, plus = pl.pallas_call(
        pack_kernel,
        out_shape=[third] * 3,
        in_specs=[HBM] * 4,
        out_specs=[VM] * 3,
        scratch_shapes=[
            pltpu.SMEM((offsets.shape[0],), jnp.int32),
            pltpu.VMEM(offsets.shape, f32),
            pltpu.VMEM(widths.shape, f32),
            pltpu.VMEM(solvation.shape, f32),
            pltpu.VMEM((27, 8, 128), f32),
            pltpu.SMEM((9,), jnp.int32),
            pltpu.SemaphoreType.DMA((4,)),
        ],
        compiler_params=pltpu.CompilerParams(vmem_limit_bytes=60 * 1024 * 1024),
        name="pack",
    )(heading[:, 0], offsets, widths, solvation)
    left_in, right_in = passed_along(plus, "gy", 1), passed_along(minus, "gy", -1)
    begun = field("stored", depth, 4, [[(0, 0)], [(0, 1)], [(0, 2)]], [same])
    left_in, right_in, *begun = lax.optimization_barrier((left_in, right_in, *begun))
    own = jnp.concatenate([same, left_in, right_in], axis=1)
    count = lax.axis_size("gx")
    partner = lax.ppermute(own, "gx", [(r, r + 1 - 2 * (r % 2)) for r in range(count)])
    even = lax.rem(lax.axis_index("gx"), 2) == 0
    none = jnp.zeros_like(own[0])
    far = jnp.where(
        even,
        jnp.stack([own[2], partner[1], partner[2]]),
        jnp.stack([own[0], partner[1], partner[0]]),
    )
    near = jnp.where(even, own[0:1], own[2:3])
    ahead = [(r, r + 2 - 4 * (r % 2)) for r in range(count)]
    behind = [(r, r - 2 + 4 * (r % 2)) for r in range(count)]
    far = lax.ppermute(far, "gx", [p for p in ahead if 0 <= p[1] < count])
    near = lax.ppermute(near, "gx", [p for p in behind if 0 <= p[1] < count])
    beside = jnp.stack(
        [
            jnp.where(even, none, partner[1]),
            jnp.where(even, partner[0], partner[2]),
            jnp.where(even, partner[1], none),
        ]
    )
    begun = field(
        "chip", depth, 16, [[(0, g), (1, g), (2, g)] for g in range(3)],
        [left_in, right_in, beside], begun,
    )
    far, near, *begun = lax.optimization_barrier((far, near, *begun))
    one = jnp.concatenate([near, jnp.zeros_like(near)])
    above, below = jnp.where(even, far[0:2], one), jnp.where(even, one, far[0:2])
    core, left, right = field(
        "rest", depth, 16, [[(0, 0), (0, 1)], [(2, 2)], [(1, 0), (1, 1)]],
        [above, below, far], begun,
    )
    from_left = passed_along(right, "gy", 1)
    from_right = passed_along(left, "gy", -1)
    return pl.pallas_call(
        edge_kernel,
        out_shape=jax.ShapeDtypeStruct(old_map.shape, f32),
        in_specs=[VM] * 4,
        out_specs=VM,
        compiler_params=small,
        name="edges",
    )(core.reshape(old_map.shape), old_map, from_left, from_right)


def solution(mesh):
    placed = (
        P(("gx", "gy"), None, None),
        P(("gx", "gy"), None),
        P(("gx", "gy"), None),
        P(("gx", "gy"), None),
        P("gx", "gy", None),
    )
    return jax.shard_map(
        body, mesh=mesh, in_specs=placed, out_specs=P("gx", "gy", None), check_vma=False
    )
```

```python
import functools
import jax
import jax.numpy as jnp
from jax import lax
from jax.experimental import pallas as pl
from jax.experimental.pallas import tpu as pltpu
from jax.sharding import PartitionSpec as P

LOG2E = 1.4426950408889634
FAR = 1.0e6
W = 5
f32, bf16 = jnp.float32, jnp.bfloat16
ABOVE, OWN, BELOW = 0, 1, 2
CORE_ROWS = (128, 192, 128)
EDGE_ROWS = (64, 80, 64)


def quotient(n, d):
    return lax.shift_right_logical(n * ((65536 + d - 1) // d), 16)


def put_rows(ti, tj, start, group, core):
    n = (CORE_ROWS if core else EDGE_ROWS)[group]
    m = lax.broadcasted_iota(jnp.int32, (n, 128), 0)
    if core:
        row = m + (64 if group == BELOW else 0)
        i = quotient(row, 24)
        j = row - i * 24
    else:
        side = m >= n // 2
        e = jnp.where(side, m - n // 2, m) + (8 if group == BELOW else 0)
        i = quotient(e, 5)
        j = e - i * 5 + jnp.where(side, 24, -W)
    place = (i + (8, 0, -8)[group]).astype(f32)
    if group == ABOVE:
        place = jnp.where(i >= W, FAR, place)
    if group == BELOW:
        place = jnp.where(i < 8 - W, FAR, place)
    ti[start:start + n, :] = place
    tj[start:start + n, :] = j.astype(f32)


def split(v):
    h = v.astype(bf16)
    return h, (v - h.astype(f32)).astype(bf16)


def compact(place, sources, shift, count):
    row = lax.broadcasted_iota(jnp.int32, (8, 128), 0)
    for ref, part in sources:
        bits = jnp.zeros((1, 128), f32)
        for s in range(ref.shape[1]):
            bits = bits + ref[part, s, 5:6, :] * float(1 << s)
        mask = jnp.max(bits).astype(jnp.int32)
        for s in range(ref.shape[1]):
            place[count] = jnp.where(row == 6, shift, ref[part, s])
            count = count + (lax.shift_right_logical(mask, s) & 1)
    return count


def fill_up(place, count, blocks):
    row = lax.broadcasted_iota(jnp.int32, (8, 128), 0)
    dead = jnp.where(row == 3, 1.0, 0.0).astype(f32)
    for s in range(blocks - 1):
        place[count + s] = dead


def add_field(lists, counts, ti, tj, rows, starts, adds, depth, blocks, wide):
    k_io = lax.broadcasted_iota(jnp.int32, (1, wide), 1).astype(f32)
    dot = functools.partial(jnp.dot, preferred_element_type=f32)

    def stage(g, at, blocks):
        n = rows[g]
        recs = [lists[g, at + q] for q in range(blocks)]
        rec = jnp.concatenate(recs, axis=1)
        x, y, weight = rec[0:1] * 8.0, rec[1:2] * 24.0, rec[4:5]
        c = (-0.5 * LOG2E) / (rec[3:4] * rec[3:4])
        ri, rj = ti[starts[g]:starts[g] + n, :], tj[starts[g]:starts[g] + n, :]
        dx = jnp.concatenate([ri] * blocks, axis=1) - x
        dy = jnp.concatenate([rj] * blocks, axis=1) - y
        ph, plo = split(jnp.exp2((dx * dx + dy * dy) * c) * weight)
        cols = jnp.concatenate([jnp.transpose(r) for r in recs], axis=0)
        z = cols[:, 2:3] * 1024.0
        cz = (-0.5 * LOG2E) / (cols[:, 3:4] * cols[:, 3:4])

        def along(b):
            d = k_io - (z - float(b * wide))
            return split(jnp.exp2(d * (d * cz)))

        nxt = along(0)
        for b in range(depth // wide):
            zh, zl = nxt
            if b + 1 < depth // wide:
                nxt = along(b + 1)
            r = dot(jnp.concatenate([ph, plo, ph], 1), jnp.concatenate([zh, zh, zl], 0))
            for ref, to, count, source in adds[g]:
                ref[to:to + count, b * wide:(b + 1) * wide] += r[source:source + count]

    for g in range(3):
        def step(t, carry, g=g):
            stage(g, t * blocks, blocks)
            return carry
        whole = lax.div(counts[g] + (blocks // 2 - 1), jnp.int32(blocks))
        lax.fori_loop(0, whole, step, 0)

        @pl.when(whole * blocks < counts[g])
        def _(g=g, whole=whole):
            stage(g, whole * blocks, blocks // 2)


def core_adds(ref):
    return [[(ref, 0, 128, 0)], [(ref, 0, 192, 0)], [(ref, 64, 128, 0)]]


def edge_adds(left, right):
    return [
        [(left, 0, 32, 0), (right, 0, 32, 32)],
        [(left, 0, 40, 0), (right, 0, 40, 40)],
        [(left, 8, 32, 0), (right, 8, 32, 32)],
    ]


def both_adds(core, left, right):
    return [
        a + [(ref, to, n, source + CORE_ROWS[g]) for ref, to, n, source in b]
        for g, (a, b) in enumerate(zip(core_adds(core), edge_adds(left, right)))
    ]


def prepare(ti, tj, kinds):
    rows, starts, at = [], [], 0
    for g in range(3):
        starts.append(at)
        for core in kinds:
            put_rows(ti, tj, at, g, core)
            at += (CORE_ROWS if core else EDGE_ROWS)[g]
        rows.append(at - starts[-1])
    return rows, starts


BLOCKS, WIDE = 4, 256


def field_kernel(sources, begun, outs, *refs):
    lists, ti, tj = refs[-3:]
    totals, inputs = refs[-3 - outs:-3], refs[:-3 - outs]
    depth = totals[0].shape[1]
    rows, starts = prepare(ti, tj, (True, False)[: max(1, outs - 1)])
    for n, ref in enumerate(totals):
        ref[...] = inputs[len(inputs) - outs + n][...] if begun else jnp.zeros_like(ref)
    counts = []
    for g in range(3):
        segments = [(inputs[n], part) for n, part in sources[g]]
        counts.append(compact(lists.at[g], segments, 0.0, jnp.int32(0)))
        fill_up(lists.at[g], counts[g], BLOCKS)
    adds = both_adds(*totals) if outs == 3 else core_adds(*totals)
    add_field(lists, counts, ti, tj, rows, starts, adds, depth, BLOCKS, WIDE)


def edge_field_kernel(sources, *refs):
    left, right, lists, ti, tj = refs[-5:]
    inputs = refs[:-5]
    depth = left.shape[1]
    put_rows(ti, tj, 0, OWN, False)
    left[...] = inputs[-2][...]
    right[...] = inputs[-1][...]
    count = jnp.int32(0)
    for g in range(3):
        segments = [(inputs[n], part) for n, part in sources[g]]
        count = compact(lists, segments, (-8.0, 0.0, 8.0)[g], count)
    fill_up(lists, count, 8)
    k_io = lax.broadcasted_iota(jnp.int32, (1, WIDE), 1).astype(f32)
    dot = functools.partial(jnp.dot, preferred_element_type=f32)

    def stage(at, blocks):
        recs = [lists[at + q] for q in range(blocks)]
        rec = jnp.concatenate(recs, axis=1)
        x, y, weight = rec[0:1] * 8.0, rec[1:2] * 24.0, rec[4:5]
        c = (-0.5 * LOG2E) / (rec[3:4] * rec[3:4])
        i = jnp.concatenate([ti[...]] * blocks, axis=1) - rec[6:7]
        dx = i - x
        dy = jnp.concatenate([tj[...]] * blocks, axis=1) - y
        value = jnp.exp2((dx * dx + dy * dy) * c) * weight
        ph, plo = split(jnp.where(jnp.abs(i - 3.5) < 4.0 + W, value, 0.0))
        cols = jnp.concatenate([jnp.transpose(r) for r in recs], axis=0)
        z = cols[:, 2:3] * 1024.0
        cz = (-0.5 * LOG2E) / (cols[:, 3:4] * cols[:, 3:4])

        def along(b):
            d = k_io - (z - float(b * WIDE))
            return split(jnp.exp2(d * (d * cz)))

        nxt = along(0)
        for b in range(depth // WIDE):
            zh, zl = nxt
            if b + 1 < depth // WIDE:
                nxt = along(b + 1)
            pp = dot(jnp.concatenate([ph, plo], 0), zh)
            r = pp[:80] + pp[80:] + dot(ph, zl)
            left[:, b * WIDE:(b + 1) * WIDE] += r[0:40]
            right[:, b * WIDE:(b + 1) * WIDE] += r[40:80]

    def step(t, carry):
        stage(t * 8, 8)
        return carry

    whole = lax.shift_right_logical(count + 1, 3)
    lax.fori_loop(0, whole, step, 0)
    after = count - whole * 8

    @pl.when(after > 2)
    def _():
        stage(whole * 8, 4)

    @pl.when(((after > 0) & (after <= 2)) | (after > 4))
    def _():
        stage(whole * 8 + jnp.where(after > 2, 4, 0), 2)


VM = pl.BlockSpec(memory_space=pltpu.VMEM)
HBM = pl.BlockSpec(memory_space=pltpu.HBM)


def field(name, depth, blocks, sources, arrays, begun=(), outs=3):
    operands = (*arrays, *begun)
    shapes = ((192, depth), (40, depth), (40, depth))[:outs]
    rows, place = sum(CORE_ROWS) + sum(EDGE_ROWS), (3, 27 + 2 * BLOCKS, 8, 128)
    kernel = functools.partial(field_kernel, sources, bool(begun), outs)
    if outs == 2:
        shapes, rows, place = ((40, depth),) * 2, EDGE_ROWS[OWN], (81 + 8, 8, 128)
        kernel = functools.partial(edge_field_kernel, sources)
    return pl.pallas_call(
        kernel,
        out_shape=[jax.ShapeDtypeStruct(s, f32) for s in shapes],
        in_specs=[VM] * len(operands),
        out_specs=[VM] * len(shapes),
        scratch_shapes=[
            pltpu.VMEM(place, f32),
            pltpu.VMEM((rows, 128), f32),
            pltpu.VMEM((rows, 128), f32),
        ],
        compiler_params=pltpu.CompilerParams(vmem_limit_bytes=32 * 1024 * 1024),
        cost_estimate=pl.CostEstimate(
            flops=blocks * 200_000_000, bytes_accessed=4_000_000, transcendentals=blocks * 300_000
        ),
        name=name,
    )(*operands)


def pack_kernel(*refs):
    hbm, (minus, same, plus), local, (slots, taken, sems) = refs[:4], refs[4:7], refs[7:11], refs[11:]
    fetches = [pltpu.make_async_copy(a, b, sems.at[n]) for n, (a, b) in enumerate(zip(hbm, local))]
    for fetch in fetches:
        fetch.start()
    heading, offsets, widths, solvation = local
    slots[...] = jnp.zeros_like(slots)
    for h in range(9):
        taken[h] = 0
    for fetch in fetches:
        fetch.wait()
    tile_row, tile_rows = lax.axis_index("gx"), lax.axis_size("gx")
    for b in range(offsets.shape[0]):
        h = heading[b]
        n = taken[h]
        taken[h] = n + 1
        row, col = lax.div(h, 3), lax.rem(h, 3)
        place = col * 9 + row * 3 + n
        slots[place, 0:3, :] = offsets[b]
        slots[place, 3:4, :] = widths[b:b + 1, :]
        slots[place, 4:5, :] = solvation[b:b + 1, :]
        home = tile_row + row - 1
        inside = (home >= 0) & (home < tile_rows)
        slots[place, 5:6, :] = jnp.full((1, 128), jnp.where(inside, 1.0, 0.0), f32)
    for k, out in enumerate((minus, same, plus)):
        out[...] = slots[9 * k:9 * k + 9].reshape(out.shape)


def edge_kernel(core, old, from_left, from_right, out):
    out[...] = core[...] + old[...]
    for i in range(core.shape[0]):
        out[i, 0:5, :] += from_left[i * 5:i * 5 + 5, :]
        out[i, 19:24, :] += from_right[i * 5:i * 5 + 5, :]


def passed_along(value, axis, steps):
    count = lax.axis_size(axis)
    first, last = (max(0, -steps), min(count, count - steps))
    return lax.ppermute(value, axis, [(source, source + steps) for source in range(first, last)])


def body(offsets, widths, solvation, heading, old_map):
    depth = old_map.shape[2]
    third = jax.ShapeDtypeStruct((3, 3, 8, 128), f32)
    small = pltpu.CompilerParams(vmem_limit_bytes=8 * 1024 * 1024)
    minus, same, plus = pl.pallas_call(
        pack_kernel,
        out_shape=[third] * 3,
        in_specs=[HBM] * 4,
        out_specs=[VM] * 3,
        scratch_shapes=[
            pltpu.SMEM((offsets.shape[0],), jnp.int32),
            pltpu.VMEM(offsets.shape, f32),
            pltpu.VMEM(widths.shape, f32),
            pltpu.VMEM(solvation.shape, f32),
            pltpu.VMEM((27, 8, 128), f32),
            pltpu.SMEM((9,), jnp.int32),
            pltpu.SemaphoreType.DMA((4,)),
        ],
        compiler_params=pltpu.CompilerParams(vmem_limit_bytes=60 * 1024 * 1024),
        name="pack",
    )(heading[:, 0], offsets, widths, solvation)
    left_in, right_in = passed_along(plus, "gy", 1), passed_along(minus, "gy", -1)
    begun = field("stored", depth, 4, [[(0, 0)], [(0, 1)], [(0, 2)]], [same])
    left_in, right_in, *begun = lax.optimization_barrier((left_in, right_in, *begun))
    own = jnp.concatenate([same, left_in, right_in], axis=1)
    count = lax.axis_size("gx")
    partner = lax.ppermute(own, "gx", [(r, r + 1 - 2 * (r % 2)) for r in range(count)])
    even = lax.rem(lax.axis_index("gx"), 2) == 0
    none = jnp.zeros_like(own[0])
    far = jnp.where(
        even,
        jnp.stack([own[2], partner[1], partner[2]]),
        jnp.stack([own[0], partner[1], partner[0]]),
    )
    near = jnp.where(even, own[0:1], own[2:3])
    ahead = [(r, r + 2 - 4 * (r % 2)) for r in range(count)]
    behind = [(r, r - 2 + 4 * (r % 2)) for r in range(count)]
    far = lax.ppermute(far, "gx", [p for p in ahead if 0 <= p[1] < count])
    near = lax.ppermute(near, "gx", [p for p in behind if 0 <= p[1] < count])
    beside = jnp.stack(
        [
            jnp.where(even, none, partner[1]),
            jnp.where(even, partner[0], partner[2]),
            jnp.where(even, partner[1], none),
        ]
    )
    begun = field(
        "chip", depth, 16, [[(0, g), (1, g), (2, g)] for g in range(3)],
        [left_in, right_in, beside], begun,
    )
    far, near, *begun = lax.optimization_barrier((far, near, *begun))
    one = jnp.concatenate([near, jnp.zeros_like(near)])
    above, below = jnp.where(even, far[0:2], one), jnp.where(even, one, far[0:2])
    sources, arrays = [[(0, 0), (0, 1)], [(2, 2)], [(1, 0), (1, 1)]], [above, below, far]
    left, right = field("rest_edges", depth, 16, sources, arrays, begun[1:], 2)
    from_left, from_right = passed_along(right, "gy", 1), passed_along(left, "gy", -1)
    (core,) = field("rest_core", depth, 16, sources, arrays, begun[:1], 1)
    core, from_left, from_right = lax.optimization_barrier((core, from_left, from_right))
    return pl.pallas_call(
        edge_kernel,
        out_shape=jax.ShapeDtypeStruct(old_map.shape, f32),
        in_specs=[VM] * 4,
        out_specs=VM,
        compiler_params=small,
        name="edges",
    )(core.reshape(old_map.shape), old_map, from_left, from_right)


def solution(mesh):
    placed = (
        P(("gx", "gy"), None, None),
        P(("gx", "gy"), None),
        P(("gx", "gy"), None),
        P(("gx", "gy"), None),
        P("gx", "gy", None),
    )
    return jax.shard_map(
        body, mesh=mesh, in_specs=placed, out_specs=P("gx", "gy", None), check_vma=False
    )
```

```python
import functools
import jax
import jax.numpy as jnp
from jax import lax
from jax.experimental import pallas as pl
from jax.experimental.pallas import tpu as pltpu
from jax.sharding import PartitionSpec as P

LOG2E = 1.4426950408889634
FAR = 1.0e6
W = 5
f32, bf16 = jnp.float32, jnp.bfloat16
ABOVE, OWN, BELOW = 0, 1, 2
CORE_ROWS = (128, 192, 128)
EDGE_ROWS = (64, 80, 64)


def quotient(n, d):
    return lax.shift_right_logical(n * ((65536 + d - 1) // d), 16)


def put_rows(ti, tj, start, group, core):
    n = (CORE_ROWS if core else EDGE_ROWS)[group]
    m = lax.broadcasted_iota(jnp.int32, (n, 128), 0)
    if core:
        row = m + (64 if group == BELOW else 0)
        i = quotient(row, 24)
        j = row - i * 24
    else:
        side = m >= n // 2
        e = jnp.where(side, m - n // 2, m) + (8 if group == BELOW else 0)
        i = quotient(e, 5)
        right = jnp.logical_xor(side, lax.rem(lax.axis_index("gy"), 2) == 0)
        j = e - i * 5 + jnp.where(right, 24, -W)
    place = (i + (8, 0, -8)[group]).astype(f32)
    if group == ABOVE:
        place = jnp.where(i >= W, FAR, place)
    if group == BELOW:
        place = jnp.where(i < 8 - W, FAR, place)
    ti[start:start + n, :] = place
    tj[start:start + n, :] = j.astype(f32)


def split(v):
    h = v.astype(bf16)
    return h, (v - h.astype(f32)).astype(bf16)


def compact(place, sources, shift, count):
    row = lax.broadcasted_iota(jnp.int32, (8, 128), 0)
    for ref, part in sources:
        bits = jnp.zeros((1, 128), f32)
        for s in range(ref.shape[1]):
            bits = bits + ref[part, s, 5:6, :] * float(1 << s)
        mask = jnp.max(bits).astype(jnp.int32)
        for s in range(ref.shape[1]):
            place[count] = jnp.where(row == 6, shift, ref[part, s])
            count = count + (lax.shift_right_logical(mask, s) & 1)
    return count


def fill_up(place, count, blocks):
    row = lax.broadcasted_iota(jnp.int32, (8, 128), 0)
    dead = jnp.where(row == 3, 1.0, 0.0).astype(f32)
    for s in range(blocks - 1):
        place[count + s] = dead


def add_field(lists, counts, ti, tj, rows, starts, adds, depth, blocks, wide):
    k_io = lax.broadcasted_iota(jnp.int32, (1, wide), 1).astype(f32)
    dot = functools.partial(jnp.dot, preferred_element_type=f32)

    def stage(g, at, blocks):
        n = rows[g]
        recs = [lists[g, at + q] for q in range(blocks)]
        rec = jnp.concatenate(recs, axis=1)
        x, y, weight = rec[0:1] * 8.0, rec[1:2] * 24.0, rec[4:5]
        c = (-0.5 * LOG2E) / (rec[3:4] * rec[3:4])
        ri, rj = ti[starts[g]:starts[g] + n, :], tj[starts[g]:starts[g] + n, :]
        dx = jnp.concatenate([ri] * blocks, axis=1) - x
        dy = jnp.concatenate([rj] * blocks, axis=1) - y
        ph, plo = split(jnp.exp2((dx * dx + dy * dy) * c) * weight)
        cols = jnp.concatenate([jnp.transpose(r) for r in recs], axis=0)
        z = cols[:, 2:3] * 1024.0
        cz = (-0.5 * LOG2E) / (cols[:, 3:4] * cols[:, 3:4])

        def along(b):
            d = k_io - (z - float(b * wide))
            return split(jnp.exp2(d * (d * cz)))

        nxt = along(0)
        for b in range(depth // wide):
            zh, zl = nxt
            if b + 1 < depth // wide:
                nxt = along(b + 1)
            r = dot(jnp.concatenate([ph, plo, ph], 1), jnp.concatenate([zh, zh, zl], 0))
            for ref, to, count, source in adds[g]:
                ref[to:to + count, b * wide:(b + 1) * wide] += r[source:source + count]

    for g in range(3):
        def step(t, carry, g=g):
            stage(g, t * blocks, blocks)
            return carry
        whole = lax.div(counts[g] + (blocks // 2 - 1), jnp.int32(blocks))
        lax.fori_loop(0, whole, step, 0)

        @pl.when(whole * blocks < counts[g])
        def _(g=g, whole=whole):
            stage(g, whole * blocks, blocks // 2)


def core_adds(ref):
    return [[(ref, 0, 128, 0)], [(ref, 0, 192, 0)], [(ref, 64, 128, 0)]]


def edge_adds(first, second):
    return [
        [(first, 0, 32, 0), (second, 0, 32, 32)],
        [(first, 0, 40, 0), (second, 0, 40, 40)],
        [(first, 8, 32, 0), (second, 8, 32, 32)],
    ]


def both_adds(core, first, second):
    return [
        a + [(ref, to, n, source + CORE_ROWS[g]) for ref, to, n, source in b]
        for g, (a, b) in enumerate(zip(core_adds(core), edge_adds(first, second)))
    ]


def prepare(ti, tj, kinds):
    rows, starts, at = [], [], 0
    for g in range(3):
        starts.append(at)
        for core in kinds:
            put_rows(ti, tj, at, g, core)
            at += (CORE_ROWS if core else EDGE_ROWS)[g]
        rows.append(at - starts[-1])
    return rows, starts


BLOCKS, WIDE = 4, 256


def field_kernel(sources, begun, outs, *refs):
    lists, ti, tj = refs[-3:]
    totals, inputs = refs[-3 - outs:-3], refs[:-3 - outs]
    depth = totals[0].shape[1]
    rows, starts = prepare(ti, tj, (True, False)[: max(1, outs - 1)])
    for n, ref in enumerate(totals):
        ref[...] = inputs[len(inputs) - outs + n][...] if begun else jnp.zeros_like(ref)
    counts = []
    for g in range(3):
        segments = [(inputs[n], part) for n, part in sources[g]]
        counts.append(compact(lists.at[g], segments, 0.0, jnp.int32(0)))
        fill_up(lists.at[g], counts[g], BLOCKS)
    adds = both_adds(*totals) if outs == 3 else core_adds(*totals)
    add_field(lists, counts, ti, tj, rows, starts, adds, depth, BLOCKS, WIDE)


def edge_field_kernel(sources, *refs):
    first, second, lists, ti, tj = refs[-5:]
    inputs = refs[:-5]
    depth = first.shape[1]
    put_rows(ti, tj, 0, OWN, False)
    first[...] = inputs[-2][...]
    second[...] = inputs[-1][...]
    count = jnp.int32(0)
    for g in range(3):
        segments = [(inputs[n], part) for n, part in sources[g]]
        count = compact(lists, segments, (-8.0, 0.0, 8.0)[g], count)
    fill_up(lists, count, 8)
    k_io = lax.broadcasted_iota(jnp.int32, (1, WIDE), 1).astype(f32)
    dot = functools.partial(jnp.dot, preferred_element_type=f32)

    def stage(at, blocks):
        recs = [lists[at + q] for q in range(blocks)]
        rec = jnp.concatenate(recs, axis=1)
        x, y, weight = rec[0:1] * 8.0, rec[1:2] * 24.0, rec[4:5]
        c = (-0.5 * LOG2E) / (rec[3:4] * rec[3:4])
        i = jnp.concatenate([ti[...]] * blocks, axis=1) - rec[6:7]
        dx = i - x
        dy = jnp.concatenate([tj[...]] * blocks, axis=1) - y
        value = jnp.exp2((dx * dx + dy * dy) * c) * weight
        ph, plo = split(jnp.where(jnp.abs(i - 3.5) < 4.0 + W, value, 0.0))
        cols = jnp.concatenate([jnp.transpose(r) for r in recs], axis=0)
        z = cols[:, 2:3] * 1024.0
        cz = (-0.5 * LOG2E) / (cols[:, 3:4] * cols[:, 3:4])

        def along(b):
            d = k_io - (z - float(b * WIDE))
            return split(jnp.exp2(d * (d * cz)))

        nxt = along(0)
        for b in range(depth // WIDE):
            zh, zl = nxt
            if b + 1 < depth // WIDE:
                nxt = along(b + 1)
            pp = dot(jnp.concatenate([ph, plo], 0), zh)
            r = pp[:80] + pp[80:] + dot(ph, zl)
            first[:, b * WIDE:(b + 1) * WIDE] += r[0:40]
            second[:, b * WIDE:(b + 1) * WIDE] += r[40:80]

    def step(t, carry):
        stage(t * 8, 8)
        return carry

    whole = lax.shift_right_logical(count + 1, 3)
    lax.fori_loop(0, whole, step, 0)
    after = count - whole * 8

    @pl.when(after > 2)
    def _():
        stage(whole * 8, 4)

    @pl.when(((after > 0) & (after <= 2)) | (after > 4))
    def _():
        stage(whole * 8 + jnp.where(after > 2, 4, 0), 2)


VM = pl.BlockSpec(memory_space=pltpu.VMEM)
HBM = pl.BlockSpec(memory_space=pltpu.HBM)


def field(name, depth, blocks, sources, arrays, begun=(), outs=3):
    operands = (*arrays, *begun)
    shapes = ((192, depth), (40, depth), (40, depth))[:outs]
    rows, place = sum(CORE_ROWS) + sum(EDGE_ROWS), (3, 27 + 2 * BLOCKS, 8, 128)
    kernel = functools.partial(field_kernel, sources, bool(begun), outs)
    if outs == 2:
        shapes, rows, place = ((40, depth),) * 2, EDGE_ROWS[OWN], (81 + 8, 8, 128)
        kernel = functools.partial(edge_field_kernel, sources)
    return pl.pallas_call(
        kernel,
        out_shape=[jax.ShapeDtypeStruct(s, f32) for s in shapes],
        in_specs=[VM] * len(operands),
        out_specs=[VM] * len(shapes),
        scratch_shapes=[
            pltpu.VMEM(place, f32),
            pltpu.VMEM((rows, 128), f32),
            pltpu.VMEM((rows, 128), f32),
        ],
        compiler_params=pltpu.CompilerParams(vmem_limit_bytes=32 * 1024 * 1024),
        cost_estimate=pl.CostEstimate(
            flops=blocks * 200_000_000, bytes_accessed=4_000_000, transcendentals=blocks * 300_000
        ),
        name=name,
    )(*operands)


def pack_kernel(*refs):
    hbm, (pair_out, same, other_out), local, (slots, taken, sems) = refs[:4], refs[4:7], refs[7:11], refs[11:]
    fetches = [pltpu.make_async_copy(a, b, sems.at[n]) for n, (a, b) in enumerate(zip(hbm, local))]
    for fetch in fetches:
        fetch.start()
    heading, offsets, widths, solvation = local
    slots[...] = jnp.zeros_like(slots)
    for h in range(9):
        taken[h] = 0
    for fetch in fetches:
        fetch.wait()
    tile_row, tile_rows = lax.axis_index("gx"), lax.axis_size("gx")
    for b in range(offsets.shape[0]):
        h = heading[b]
        n = taken[h]
        taken[h] = n + 1
        row, col = lax.div(h, 3), lax.rem(h, 3)
        place = col * 9 + row * 3 + n
        slots[place, 0:3, :] = offsets[b]
        slots[place, 3:4, :] = widths[b:b + 1, :]
        slots[place, 4:5, :] = solvation[b:b + 1, :]
        home = tile_row + row - 1
        inside = (home >= 0) & (home < tile_rows)
        slots[place, 5:6, :] = jnp.full((1, 128), jnp.where(inside, 1.0, 0.0), f32)
    even = lax.rem(lax.axis_index("gy"), 2) == 0
    for k, out in ((jnp.where(even, 2, 0), pair_out), (1, same), (jnp.where(even, 0, 2), other_out)):
        out[...] = slots[pl.ds(9 * k, 9)].reshape(out.shape)


def edge_kernel(core, old, first, second, out):
    out[...] = core[...] + old[...]
    even = lax.rem(lax.axis_index("gy"), 2) == 0

    def add(from_left, from_right):
        for i in range(core.shape[0]):
            out[i, 0:5, :] += from_left[i * 5:i * 5 + 5, :]
            out[i, 19:24, :] += from_right[i * 5:i * 5 + 5, :]

    @pl.when(even)
    def _():
        add(second, first)

    @pl.when(jnp.logical_not(even))
    def _():
        add(first, second)


def swapped(value, start):
    pairs = [(k, k + 1) for k in range(start, lax.axis_size("gy") - 1, 2)]
    return lax.ppermute(value, "gy", pairs + [(b, a) for a, b in pairs])


def body(offsets, widths, solvation, heading, old_map):
    depth = old_map.shape[2]
    third = jax.ShapeDtypeStruct((3, 3, 8, 128), f32)
    small = pltpu.CompilerParams(vmem_limit_bytes=8 * 1024 * 1024)
    first, same, second = pl.pallas_call(
        pack_kernel,
        out_shape=[third] * 3,
        in_specs=[HBM] * 4,
        out_specs=[VM] * 3,
        scratch_shapes=[
            pltpu.SMEM((offsets.shape[0],), jnp.int32),
            pltpu.VMEM(offsets.shape, f32),
            pltpu.VMEM(widths.shape, f32),
            pltpu.VMEM(solvation.shape, f32),
            pltpu.VMEM((27, 8, 128), f32),
            pltpu.SMEM((9,), jnp.int32),
            pltpu.SemaphoreType.DMA((4,)),
        ],
        compiler_params=pltpu.CompilerParams(vmem_limit_bytes=60 * 1024 * 1024),
        name="pack",
    )(heading[:, 0], offsets, widths, solvation)
    first, second = swapped(first, 0), swapped(second, 1)
    begun = field("stored", depth, 4, [[(0, 0)], [(0, 1)], [(0, 2)]], [same])
    first, second, *begun = lax.optimization_barrier((first, second, *begun))
    own = jnp.concatenate([same, first, second], axis=1)
    count = lax.axis_size("gx")
    partner = lax.ppermute(own, "gx", [(r, r + 1 - 2 * (r % 2)) for r in range(count)])
    even = lax.rem(lax.axis_index("gx"), 2) == 0
    none = jnp.zeros_like(own[0])
    far = jnp.where(
        even,
        jnp.stack([own[2], partner[1], partner[2]]),
        jnp.stack([own[0], partner[1], partner[0]]),
    )
    near = jnp.where(even, own[0:1], own[2:3])
    ahead = [(r, r + 2 - 4 * (r % 2)) for r in range(count)]
    behind = [(r, r - 2 + 4 * (r % 2)) for r in range(count)]
    far = lax.ppermute(far, "gx", [p for p in ahead if 0 <= p[1] < count])
    near = lax.ppermute(near, "gx", [p for p in behind if 0 <= p[1] < count])
    beside = jnp.stack(
        [
            jnp.where(even, none, partner[1]),
            jnp.where(even, partner[0], partner[2]),
            jnp.where(even, partner[1], none),
        ]
    )
    begun = field(
        "chip", depth, 16, [[(0, g), (1, g), (2, g)] for g in range(3)],
        [first, second, beside], begun,
    )
    far, near, *begun = lax.optimization_barrier((far, near, *begun))
    one = jnp.concatenate([near, jnp.zeros_like(near)])
    above, below = jnp.where(even, far[0:2], one), jnp.where(even, one, far[0:2])
    sources, arrays = [[(0, 0), (0, 1)], [(2, 2)], [(1, 0), (1, 1)]], [above, below, far]
    edges = field("rest_edges", depth, 16, sources, arrays, begun[1:], 2)
    first, second = swapped(edges[0], 0), swapped(edges[1], 1)
    (core,) = field("rest_core", depth, 16, sources, arrays, begun[:1], 1)
    core, first, second = lax.optimization_barrier((core, first, second))
    return pl.pallas_call(
        edge_kernel,
        out_shape=jax.ShapeDtypeStruct(old_map.shape, f32),
        in_specs=[VM] * 4,
        out_specs=VM,
        compiler_params=small,
        name="edges",
    )(core.reshape(old_map.shape), old_map, first, second)


def solution(mesh):
    placed = (
        P(("gx", "gy"), None, None),
        P(("gx", "gy"), None),
        P(("gx", "gy"), None),
        P(("gx", "gy"), None),
        P("gx", "gy", None),
    )
    return jax.shard_map(
        body, mesh=mesh, in_specs=placed, out_specs=P("gx", "gy", None), check_vma=False
    )
```

```python
import functools
import jax
import jax.numpy as jnp
from jax import lax
from jax.experimental import pallas as pl
from jax.experimental.pallas import tpu as pltpu
from jax.sharding import PartitionSpec as P

LOG2E = 1.4426950408889634
FAR = 1.0e6
W = 5
f32, bf16 = jnp.float32, jnp.bfloat16
ABOVE, OWN, BELOW = 0, 1, 2
CORE_ROWS = (128, 192, 128)
EDGE_ROWS = (64, 80, 64)


def quotient(n, d):
    return lax.shift_right_logical(n * ((65536 + d - 1) // d), 16)


def put_rows(ti, tj, start, group, core):
    n = (CORE_ROWS if core else EDGE_ROWS)[group]
    if core:
        inner = lax.broadcasted_iota(jnp.int32, (8, 128), 0).astype(f32)
        for v in range(n // 8):
            i, part = divmod(v + (8 if group == BELOW else 0), 3)
            dead = (group == ABOVE and i >= W) or (group == BELOW and i < 8 - W)
            place = FAR if dead else float(i + (8, 0, -8)[group])
            ti[start + v * 8:start + v * 8 + 8, :] = jnp.full((8, 128), place, f32)
            tj[start + v * 8:start + v * 8 + 8, :] = inner + 8.0 * part
        return
    m = lax.broadcasted_iota(jnp.int32, (n, 128), 0)
    side = m >= n // 2
    e = jnp.where(side, m - n // 2, m) + (8 if group == BELOW else 0)
    i = quotient(e, 5)
    right = jnp.logical_xor(side, lax.rem(lax.axis_index("gy"), 2) == 0)
    j = e - i * 5 + jnp.where(right, 24, -W)
    place = (i + (8, 0, -8)[group]).astype(f32)
    if group == ABOVE:
        place = jnp.where(i >= W, FAR, place)
    if group == BELOW:
        place = jnp.where(i < 8 - W, FAR, place)
    ti[start:start + n, :] = place
    tj[start:start + n, :] = j.astype(f32)


def split(v):
    h = v.astype(bf16)
    return h, (v - h.astype(f32)).astype(bf16)


def masks(sources):
    found = []
    for ref, part in sources:
        bits = jnp.zeros((1, 128), f32)
        for s in range(ref.shape[1]):
            bits = bits + ref[part, s, 5:6, :] * float(1 << s)
        found.append(jnp.max(bits).astype(jnp.int32))
    return found


def compact(place, sources, present, shift, count):
    row = lax.broadcasted_iota(jnp.int32, (8, 128), 0)
    for (ref, part), mask in zip(sources, present):
        for s in range(ref.shape[1]):
            place[count] = jnp.where(row == 6, shift, ref[part, s]) if shift else ref[part, s]
            count = count + (lax.shift_right_logical(mask, s) & 1)
    return count


def fill_up(place, count, blocks):
    row = lax.broadcasted_iota(jnp.int32, (8, 128), 0)
    dead = jnp.where(row == 3, 1.0, 0.0).astype(f32)
    for s in range(blocks - 1):
        place[count + s] = dead


def add_field(lists, counts, ti, tj, rows, starts, adds, depth, blocks, wide):
    k_io = lax.broadcasted_iota(jnp.int32, (1, wide), 1).astype(f32)
    dot = functools.partial(jnp.dot, preferred_element_type=f32)

    def stage(g, at, blocks):
        n = rows[g]
        recs = [lists[g, at + q] for q in range(blocks)]
        rec = jnp.concatenate(recs, axis=1)
        x, y, weight = rec[0:1] * 8.0, rec[1:2] * 24.0, rec[4:5]
        c = (-0.5 * LOG2E) / (rec[3:4] * rec[3:4])
        ri, rj = ti[starts[g]:starts[g] + n, :], tj[starts[g]:starts[g] + n, :]
        dx = jnp.concatenate([ri] * blocks, axis=1) - x
        dy = jnp.concatenate([rj] * blocks, axis=1) - y
        ph, plo = split(jnp.exp2((dx * dx + dy * dy) * c) * weight)
        cols = jnp.concatenate([jnp.transpose(r) for r in recs], axis=0)
        z = cols[:, 2:3] * 1024.0
        cz = (-0.5 * LOG2E) / (cols[:, 3:4] * cols[:, 3:4])

        def along(b):
            d = k_io - (z - float(b * wide))
            return split(jnp.exp2(d * (d * cz)))

        nxt = along(0)
        for b in range(depth // wide):
            zh, zl = nxt
            if b + 1 < depth // wide:
                nxt = along(b + 1)
            r = dot(jnp.concatenate([ph, plo, ph], 1), jnp.concatenate([zh, zh, zl], 0))
            for ref, to, count, source in adds[g]:
                ref[to:to + count, b * wide:(b + 1) * wide] += r[source:source + count]

    def together(t, carry):
        for g in range(3):
            stage(g, t * blocks, blocks)
        return carry

    parts = [lax.div(c + blocks // 2, jnp.int32(blocks)) for c in counts]
    joint = jnp.minimum(jnp.minimum(parts[0], parts[1]), parts[2])
    lax.fori_loop(0, joint, together, 0)
    for g in range(3):
        begin = joint * blocks
        left = jnp.maximum(counts[g] - begin, 0)
        whole = lax.div(left + (blocks // 2 - 1), jnp.int32(blocks))

        def step(t, carry, g=g, begin=begin):
            stage(g, begin + t * blocks, blocks)
            return carry

        lax.fori_loop(0, whole, step, 0)

        @pl.when(whole * blocks < left)
        def _(g=g, at=begin + whole * blocks):
            stage(g, at, blocks // 2)


def core_adds(ref):
    return [[(ref, 0, 128, 0)], [(ref, 0, 192, 0)], [(ref, 64, 128, 0)]]


def edge_adds(first, second):
    return [
        [(first, 0, 32, 0), (second, 0, 32, 32)],
        [(first, 0, 40, 0), (second, 0, 40, 40)],
        [(first, 8, 32, 0), (second, 8, 32, 32)],
    ]


def both_adds(core, first, second):
    return [
        a + [(ref, to, n, source + CORE_ROWS[g]) for ref, to, n, source in b]
        for g, (a, b) in enumerate(zip(core_adds(core), edge_adds(first, second)))
    ]


def prepare(ti, tj, kinds):
    rows, starts, at = [], [], 0
    for g in range(3):
        starts.append(at)
        for core in kinds:
            put_rows(ti, tj, at, g, core)
            at += (CORE_ROWS if core else EDGE_ROWS)[g]
        rows.append(at - starts[-1])
    return rows, starts


BLOCKS, WIDE, EDGE_WIDE = 4, 512, 256


def field_kernel(sources, begun, outs, keep, *refs):
    lists, ti, tj = refs[-3:]
    totals, inputs = refs[-3 - outs:-3], refs[:-3 - outs]
    if keep:
        inputs[-1][...] = inputs[0][...]
    depth = totals[0].shape[1]
    rows, starts = prepare(ti, tj, (True, False)[: max(1, outs - 1)])
    for n, ref in enumerate(totals):
        ref[...] = inputs[len(inputs) - outs + n][...] if begun else jnp.zeros_like(ref)
    segments = [[(inputs[n], part) for n, part in sources[g]] for g in range(3)]
    present = [masks(segments[g]) for g in range(3)]
    counts = []
    for g in range(3):
        counts.append(compact(lists.at[g], segments[g], present[g], 0.0, jnp.int32(0)))
        fill_up(lists.at[g], counts[g], BLOCKS)
    adds = both_adds(*totals) if outs == 3 else core_adds(*totals)
    add_field(lists, counts, ti, tj, rows, starts, adds, depth, BLOCKS, WIDE)


def edge_field_kernel(sources, *refs):
    first, second, lists, ti, tj = refs[-5:]
    inputs = refs[:-5]
    depth = first.shape[1]
    put_rows(ti, tj, 0, OWN, False)
    first[...] = inputs[-2][...]
    second[...] = inputs[-1][...]
    segments = [[(inputs[n], part) for n, part in sources[g]] for g in range(3)]
    present = [masks(segments[g]) for g in range(3)]
    count = jnp.int32(0)
    for g in range(3):
        count = compact(lists, segments[g], present[g], (-8.0, 0.0, 8.0)[g], count)
    fill_up(lists, count, 8)
    k_io = lax.broadcasted_iota(jnp.int32, (1, EDGE_WIDE), 1).astype(f32)
    dot = functools.partial(jnp.dot, preferred_element_type=f32)

    def stage(at, blocks):
        recs = [lists[at + q] for q in range(blocks)]
        rec = jnp.concatenate(recs, axis=1)
        x, y, weight = rec[0:1] * 8.0, rec[1:2] * 24.0, rec[4:5]
        c = (-0.5 * LOG2E) / (rec[3:4] * rec[3:4])
        i = jnp.concatenate([ti[...]] * blocks, axis=1) - rec[6:7]
        dx = i - x
        dy = jnp.concatenate([tj[...]] * blocks, axis=1) - y
        value = jnp.exp2((dx * dx + dy * dy) * c) * weight
        ph, plo = split(jnp.where(jnp.abs(i - 3.5) < 4.0 + W, value, 0.0))
        cols = jnp.concatenate([jnp.transpose(r) for r in recs], axis=0)
        z = cols[:, 2:3] * 1024.0
        cz = (-0.5 * LOG2E) / (cols[:, 3:4] * cols[:, 3:4])

        def along(b):
            d = k_io - (z - float(b * EDGE_WIDE))
            return split(jnp.exp2(d * (d * cz)))

        nxt = along(0)
        for b in range(depth // EDGE_WIDE):
            zh, zl = nxt
            if b + 1 < depth // EDGE_WIDE:
                nxt = along(b + 1)
            pp = dot(jnp.concatenate([ph, plo], 0), zh)
            r = pp[:80] + pp[80:] + dot(ph, zl)
            first[:, b * EDGE_WIDE:(b + 1) * EDGE_WIDE] += r[0:40]
            second[:, b * EDGE_WIDE:(b + 1) * EDGE_WIDE] += r[40:80]

    def step(t, carry):
        stage(t * 8, 8)
        return carry

    whole = lax.shift_right_logical(count + 1, 3)
    lax.fori_loop(0, whole, step, 0)
    after = count - whole * 8

    @pl.when(after > 2)
    def _():
        stage(whole * 8, 4)

    @pl.when(((after > 0) & (after <= 2)) | (after > 4))
    def _():
        stage(whole * 8 + jnp.where(after > 2, 4, 0), 2)


VM = pl.BlockSpec(memory_space=pltpu.VMEM)
HBM = pl.BlockSpec(memory_space=pltpu.HBM)


def field(name, depth, blocks, sources, arrays, begun=(), outs=3, keep=False):
    operands = (*arrays, *begun)
    shapes = ((192, depth), (40, depth), (40, depth))[:outs]
    rows, place = sum(CORE_ROWS) + sum(EDGE_ROWS), (3, 27 + 2 * BLOCKS, 8, 128)
    kernel = functools.partial(field_kernel, sources, bool(begun), outs, keep)
    if outs == 2:
        shapes, rows, place = ((40, depth),) * 2, EDGE_ROWS[OWN], (81 + 8, 8, 128)
        kernel = functools.partial(edge_field_kernel, sources)
    if keep:
        shapes = (arrays[0].shape, *shapes)
    return pl.pallas_call(
        kernel,
        out_shape=[jax.ShapeDtypeStruct(s, f32) for s in shapes],
        in_specs=[VM] * len(operands),
        out_specs=[VM] * len(shapes),
        scratch_shapes=[
            pltpu.VMEM(place, f32),
            pltpu.VMEM((rows, 128), f32),
            pltpu.VMEM((rows, 128), f32),
        ],
        compiler_params=pltpu.CompilerParams(vmem_limit_bytes=32 * 1024 * 1024),
        cost_estimate=pl.CostEstimate(
            flops=blocks * 200_000_000, bytes_accessed=4_000_000, transcendentals=blocks * 300_000
        ),
        name=name,
    )(*operands)


def pack_kernel(*refs):
    hbm, (pair_out, same, other_out), local, (slots, taken, sems) = refs[:4], refs[4:7], refs[7:11], refs[11:]
    fetches = [pltpu.make_async_copy(a, b, sems.at[n]) for n, (a, b) in enumerate(zip(hbm, local))]
    for fetch in fetches:
        fetch.start()
    heading, offsets, widths, solvation = local
    slots[...] = jnp.zeros_like(slots)
    for h in range(9):
        taken[h] = 0
    for fetch in fetches:
        fetch.wait()
    tile_row, tile_rows = lax.axis_index("gx"), lax.axis_size("gx")
    for b in range(offsets.shape[0]):
        h = heading[b]
        n = taken[h]
        taken[h] = n + 1
        row, col = lax.div(h, 3), lax.rem(h, 3)
        place = col * 9 + row * 3 + n
        slots[place, 0:3, :] = offsets[b]
        slots[place, 3:4, :] = widths[b:b + 1, :]
        slots[place, 4:5, :] = solvation[b:b + 1, :]
        home = tile_row + row - 1
        inside = (home >= 0) & (home < tile_rows)
        slots[place, 5:6, :] = jnp.full((1, 128), jnp.where(inside, 1.0, 0.0), f32)
    even = lax.rem(lax.axis_index("gy"), 2) == 0
    for k, out in ((jnp.where(even, 2, 0), pair_out), (1, same), (jnp.where(even, 0, 2), other_out)):
        out[...] = slots[pl.ds(9 * k, 9)].reshape(out.shape)


def edge_kernel(core, old, first, second, out):
    out[...] = core[...] + old[...]
    even = lax.rem(lax.axis_index("gy"), 2) == 0

    def add(from_left, from_right):
        for i in range(core.shape[0]):
            out[i, 0:5, :] += from_left[i * 5:i * 5 + 5, :]
            out[i, 19:24, :] += from_right[i * 5:i * 5 + 5, :]

    @pl.when(even)
    def _():
        add(second, first)

    @pl.when(jnp.logical_not(even))
    def _():
        add(first, second)


def swapped(value, start):
    pairs = [(k, k + 1) for k in range(start, lax.axis_size("gy") - 1, 2)]
    return lax.ppermute(value, "gy", pairs + [(b, a) for a, b in pairs])


def body(offsets, widths, solvation, heading, old_map):
    depth = old_map.shape[2]
    third = jax.ShapeDtypeStruct((3, 3, 8, 128), f32)
    small = pltpu.CompilerParams(vmem_limit_bytes=8 * 1024 * 1024)
    first, same, second = pl.pallas_call(
        pack_kernel,
        out_shape=[third] * 3,
        in_specs=[HBM] * 4,
        out_specs=[VM] * 3,
        scratch_shapes=[
            pltpu.SMEM((offsets.shape[0],), jnp.int32),
            pltpu.VMEM(offsets.shape, f32),
            pltpu.VMEM(widths.shape, f32),
            pltpu.VMEM(solvation.shape, f32),
            pltpu.VMEM((27, 8, 128), f32),
            pltpu.SMEM((9,), jnp.int32),
            pltpu.SemaphoreType.DMA((4,)),
        ],
        compiler_params=pltpu.CompilerParams(vmem_limit_bytes=60 * 1024 * 1024),
        name="pack",
    )(heading[:, 0], offsets, widths, solvation)
    first, second = swapped(first, 0), swapped(second, 1)
    same, *begun = field("stored", depth, 4, [[(0, 0)], [(0, 1)], [(0, 2)]], [same], keep=True)
    first, second, *begun = lax.optimization_barrier((first, second, *begun))
    own = jnp.concatenate([same, first, second], axis=1)
    count = lax.axis_size("gx")
    partner = lax.ppermute(own, "gx", [(r, r + 1 - 2 * (r % 2)) for r in range(count)])
    even = lax.rem(lax.axis_index("gx"), 2) == 0
    none = jnp.zeros_like(own[0])
    far = jnp.where(
        even,
        jnp.stack([own[2], partner[1], partner[2]]),
        jnp.stack([own[0], partner[1], partner[0]]),
    )
    near = jnp.where(even, own[0:1], own[2:3])
    ahead = [(r, r + 2 - 4 * (r % 2)) for r in range(count)]
    behind = [(r, r - 2 + 4 * (r % 2)) for r in range(count)]
    far = lax.ppermute(far, "gx", [p for p in ahead if 0 <= p[1] < count])
    near = lax.ppermute(near, "gx", [p for p in behind if 0 <= p[1] < count])
    beside = jnp.stack(
        [
            jnp.where(even, none, partner[1]),
            jnp.where(even, partner[0], partner[2]),
            jnp.where(even, partner[1], none),
        ]
    )
    begun = field(
        "chip", depth, 16, [[(0, g), (1, g), (2, g)] for g in range(3)],
        [first, second, beside], begun,
    )
    far, near, *begun = lax.optimization_barrier((far, near, *begun))
    one = jnp.concatenate([near, jnp.zeros_like(near)])
    above, below = jnp.where(even, far[0:2], one), jnp.where(even, one, far[0:2])
    sources, arrays = [[(0, 0), (0, 1)], [(2, 2)], [(1, 0), (1, 1)]], [above, below, far]
    edges = field("rest_edges", depth, 16, sources, arrays, begun[1:], 2)
    first, second = swapped(edges[0], 0), swapped(edges[1], 1)
    (core,) = field("rest_core", depth, 16, sources, arrays, begun[:1], 1)
    core, first, second = lax.optimization_barrier((core, first, second))
    return pl.pallas_call(
        edge_kernel,
        out_shape=jax.ShapeDtypeStruct(old_map.shape, f32),
        in_specs=[VM] * 4,
        out_specs=VM,
        compiler_params=small,
        name="edges",
    )(core.reshape(old_map.shape), old_map, first, second)


def solution(mesh):
    placed = (
        P(("gx", "gy"), None, None),
        P(("gx", "gy"), None),
        P(("gx", "gy"), None),
        P(("gx", "gy"), None),
        P("gx", "gy", None),
    )
    return jax.shard_map(
        body, mesh=mesh, in_specs=placed, out_specs=P("gx", "gy", None), check_vma=False
    )
```

```python
import functools
import jax
import jax.numpy as jnp
from jax import lax
from jax.experimental import pallas as pl
from jax.experimental.pallas import tpu as pltpu
from jax.sharding import PartitionSpec as P

LOG2E = 1.4426950408889634
FAR = 1.0e6
W = 5
f32, bf16 = jnp.float32, jnp.bfloat16
ABOVE, OWN, BELOW = 0, 1, 2
CORE_ROWS = (128, 192, 128)
EDGE_ROWS = (64, 80, 64)


def quotient(n, d):
    return lax.shift_right_logical(n * ((65536 + d - 1) // d), 16)


def put_rows(ti, tj, start, group, core):
    n = (CORE_ROWS if core else EDGE_ROWS)[group]
    if core:
        inner = lax.broadcasted_iota(jnp.int32, (8, 128), 0).astype(f32)
        for v in range(n // 8):
            i, part = divmod(v + (8 if group == BELOW else 0), 3)
            dead = (group == ABOVE and i >= W) or (group == BELOW and i < 8 - W)
            place = FAR if dead else float(i + (8, 0, -8)[group])
            ti[start + v * 8:start + v * 8 + 8, :] = jnp.full((8, 128), place, f32)
            tj[start + v * 8:start + v * 8 + 8, :] = inner + 8.0 * part
        return
    m = lax.broadcasted_iota(jnp.int32, (n, 128), 0)
    side = m >= n // 2
    e = jnp.where(side, m - n // 2, m) + (8 if group == BELOW else 0)
    i = quotient(e, 5)
    right = jnp.logical_xor(side, lax.rem(lax.axis_index("gy"), 2) == 0)
    j = e - i * 5 + jnp.where(right, 24, -W)
    place = (i + (8, 0, -8)[group]).astype(f32)
    if group == ABOVE:
        place = jnp.where(i >= W, FAR, place)
    if group == BELOW:
        place = jnp.where(i < 8 - W, FAR, place)
    ti[start:start + n, :] = place
    tj[start:start + n, :] = j.astype(f32)


def split(v):
    h = v.astype(bf16)
    return h, (v - h.astype(f32)).astype(bf16)


def masks(sources):
    found = []
    for ref, part in sources:
        bits = jnp.zeros((1, 128), f32)
        for s in range(ref.shape[1]):
            bits = bits + ref[part, s, 5:6, :] * float(1 << s)
        found.append(jnp.max(bits).astype(jnp.int32))
    return found


def compact(place, sources, present, shift, count):
    row = lax.broadcasted_iota(jnp.int32, (8, 128), 0)
    for (ref, part), mask in zip(sources, present):
        for s in range(ref.shape[1]):
            place[count] = jnp.where(row == 6, shift, ref[part, s]) if shift else ref[part, s]
            count = count + (lax.shift_right_logical(mask, s) & 1)
    return count


def fill_up(place, count, blocks):
    row = lax.broadcasted_iota(jnp.int32, (8, 128), 0)
    dead = jnp.where(row == 3, 1.0, 0.0).astype(f32)
    for s in range(blocks - 1):
        place[count + s] = dead


def add_field(lists, counts, ti, tj, rows, starts, adds, depth, blocks, wide):
    k_io = lax.broadcasted_iota(jnp.int32, (1, wide), 1).astype(f32)
    dot = functools.partial(jnp.dot, preferred_element_type=f32)

    def stage(g, at, blocks):
        n = rows[g]
        recs = [lists[g, at + q] for q in range(blocks)]
        rec = jnp.concatenate(recs, axis=1)
        x, y, weight = rec[0:1] * 8.0, rec[1:2] * 24.0, rec[4:5]
        c = (-0.5 * LOG2E) / (rec[3:4] * rec[3:4])
        ri, rj = ti[starts[g]:starts[g] + n, :], tj[starts[g]:starts[g] + n, :]
        dx = jnp.concatenate([ri] * blocks, axis=1) - x
        dy = jnp.concatenate([rj] * blocks, axis=1) - y
        ph, plo = split(jnp.exp2((dx * dx + dy * dy) * c) * weight)
        cols = jnp.concatenate([jnp.transpose(r) for r in recs], axis=0)
        z = cols[:, 2:3] * 1024.0
        cz = (-0.5 * LOG2E) / (cols[:, 3:4] * cols[:, 3:4])

        def along(b):
            d = k_io - (z - float(b * wide))
            return split(jnp.exp2(d * (d * cz)))

        nxt = along(0)
        for b in range(depth // wide):
            zh, zl = nxt
            if b + 1 < depth // wide:
                nxt = along(b + 1)
            r = dot(jnp.concatenate([ph, plo, ph], 1), jnp.concatenate([zh, zh, zl], 0))
            for ref, to, count, source in adds[g]:
                ref[to:to + count, b * wide:(b + 1) * wide] += r[source:source + count]

    def together(t, carry):
        for g in range(3):
            stage(g, t * blocks, blocks)
        return carry

    parts = [lax.div(c + blocks // 2, jnp.int32(blocks)) for c in counts]
    joint = jnp.minimum(jnp.minimum(parts[0], parts[1]), parts[2])
    lax.fori_loop(0, joint, together, 0)
    for g in range(3):
        begin = joint * blocks
        left = jnp.maximum(counts[g] - begin, 0)
        whole = lax.div(left + (blocks // 2 - 1), jnp.int32(blocks))

        def step(t, carry, g=g, begin=begin):
            stage(g, begin + t * blocks, blocks)
            return carry

        lax.fori_loop(0, whole, step, 0)

        @pl.when(whole * blocks < left)
        def _(g=g, at=begin + whole * blocks):
            stage(g, at, blocks // 2)


def core_adds(ref):
    return [[(ref, 0, 128, 0)], [(ref, 0, 192, 0)], [(ref, 64, 128, 0)]]


def edge_adds(first, second):
    return [
        [(first, 0, 32, 0), (second, 0, 32, 32)],
        [(first, 0, 40, 0), (second, 0, 40, 40)],
        [(first, 8, 32, 0), (second, 8, 32, 32)],
    ]


def both_adds(core, first, second):
    return [
        a + [(ref, to, n, source + CORE_ROWS[g]) for ref, to, n, source in b]
        for g, (a, b) in enumerate(zip(core_adds(core), edge_adds(first, second)))
    ]


def prepare(ti, tj, kinds):
    rows, starts, at = [], [], 0
    for g in range(3):
        starts.append(at)
        for core in kinds:
            put_rows(ti, tj, at, g, core)
            at += (CORE_ROWS if core else EDGE_ROWS)[g]
        rows.append(at - starts[-1])
    return rows, starts


BLOCKS, WIDE, EDGE_WIDE = 4, 512, 256


def field_kernel(sources, begun, outs, keep, *refs):
    lists, ti, tj = refs[-3:]
    totals, inputs = refs[-3 - outs:-3], refs[:-3 - outs]
    if keep:
        inputs[-1][...] = inputs[0][...]
    depth = totals[0].shape[1]
    rows, starts = prepare(ti, tj, (True, False)[: max(1, outs - 1)])
    for n, ref in enumerate(totals):
        ref[...] = inputs[len(inputs) - outs + n][...] if begun else jnp.zeros_like(ref)
    segments = [[(inputs[n], part) for n, part in sources[g]] for g in range(3)]
    present = [masks(segments[g]) for g in range(3)]
    counts = []
    for g in range(3):
        counts.append(compact(lists.at[g], segments[g], present[g], 0.0, jnp.int32(0)))
        fill_up(lists.at[g], counts[g], BLOCKS)
    adds = both_adds(*totals) if outs == 3 else core_adds(*totals)
    add_field(lists, counts, ti, tj, rows, starts, adds, depth, BLOCKS, WIDE)


def edge_field_kernel(sources, *refs):
    first, second, lists, ti, tj = refs[-5:]
    inputs = refs[:-5]
    depth = first.shape[1]
    put_rows(ti, tj, 0, OWN, False)
    first[...] = inputs[-2][...]
    second[...] = inputs[-1][...]
    segments = [[(inputs[n], part) for n, part in sources[g]] for g in range(3)]
    present = [masks(segments[g]) for g in range(3)]
    count = jnp.int32(0)
    for g in range(3):
        count = compact(lists, segments[g], present[g], (-8.0, 0.0, 8.0)[g], count)
    fill_up(lists, count, 8)
    k_io = lax.broadcasted_iota(jnp.int32, (1, EDGE_WIDE), 1).astype(f32)
    dot = functools.partial(jnp.dot, preferred_element_type=f32)

    def stage(at, blocks):
        recs = [lists[at + q] for q in range(blocks)]
        rec = jnp.concatenate(recs, axis=1)
        x, y, weight = rec[0:1] * 8.0, rec[1:2] * 24.0, rec[4:5]
        c = (-0.5 * LOG2E) / (rec[3:4] * rec[3:4])
        i = jnp.concatenate([ti[...]] * blocks, axis=1) - rec[6:7]
        dx = i - x
        dy = jnp.concatenate([tj[...]] * blocks, axis=1) - y
        value = jnp.exp2((dx * dx + dy * dy) * c) * weight
        ph, plo = split(jnp.where(jnp.abs(i - 3.5) < 4.0 + W, value, 0.0))
        cols = jnp.concatenate([jnp.transpose(r) for r in recs], axis=0)
        z = cols[:, 2:3] * 1024.0
        cz = (-0.5 * LOG2E) / (cols[:, 3:4] * cols[:, 3:4])

        def along(b):
            d = k_io - (z - float(b * EDGE_WIDE))
            return split(jnp.exp2(d * (d * cz)))

        nxt = along(0)
        for b in range(depth // EDGE_WIDE):
            zh, zl = nxt
            if b + 1 < depth // EDGE_WIDE:
                nxt = along(b + 1)
            pp = dot(jnp.concatenate([ph, plo], 0), zh)
            r = pp[:80] + pp[80:] + dot(ph, zl)
            first[:, b * EDGE_WIDE:(b + 1) * EDGE_WIDE] += r[0:40]
            second[:, b * EDGE_WIDE:(b + 1) * EDGE_WIDE] += r[40:80]

    def two(t, carry):
        stage(t * 16, 8)
        stage(t * 16 + 8, 8)
        return carry

    twos = lax.shift_right_logical(count + 1, 4)
    lax.fori_loop(0, twos, two, 0)
    whole = lax.shift_right_logical(count + 1, 3)

    @pl.when(whole > twos * 2)
    def _():
        stage(twos * 16, 8)

    after = count - whole * 8

    @pl.when(after > 2)
    def _():
        stage(whole * 8, 4)

    @pl.when(((after > 0) & (after <= 2)) | (after > 4))
    def _():
        stage(whole * 8 + jnp.where(after > 2, 4, 0), 2)


VM = pl.BlockSpec(memory_space=pltpu.VMEM)
HBM = pl.BlockSpec(memory_space=pltpu.HBM)


def field(name, depth, blocks, sources, arrays, begun=(), outs=3, keep=False):
    operands = (*arrays, *begun)
    shapes = ((192, depth), (40, depth), (40, depth))[:outs]
    rows, place = sum(CORE_ROWS) + sum(EDGE_ROWS), (3, 27 + 2 * BLOCKS, 8, 128)
    kernel = functools.partial(field_kernel, sources, bool(begun), outs, keep)
    if outs == 2:
        shapes, rows, place = ((40, depth),) * 2, EDGE_ROWS[OWN], (81 + 8, 8, 128)
        kernel = functools.partial(edge_field_kernel, sources)
    if keep:
        shapes = (arrays[0].shape, *shapes)
    return pl.pallas_call(
        kernel,
        out_shape=[jax.ShapeDtypeStruct(s, f32) for s in shapes],
        in_specs=[VM] * len(operands),
        out_specs=[VM] * len(shapes),
        scratch_shapes=[
            pltpu.VMEM(place, f32),
            pltpu.VMEM((rows, 128), f32),
            pltpu.VMEM((rows, 128), f32),
        ],
        compiler_params=pltpu.CompilerParams(vmem_limit_bytes=32 * 1024 * 1024),
        cost_estimate=pl.CostEstimate(
            flops=blocks * 200_000_000, bytes_accessed=4_000_000, transcendentals=blocks * 300_000
        ),
        name=name,
    )(*operands)


def pack_kernel(*refs):
    hbm, (pair_out, same, other_out), local, (slots, taken, sems) = refs[:4], refs[4:7], refs[7:11], refs[11:]
    fetches = [pltpu.make_async_copy(a, b, sems.at[n]) for n, (a, b) in enumerate(zip(hbm, local))]
    for fetch in fetches:
        fetch.start()
    heading, offsets, widths, solvation = local
    slots[...] = jnp.zeros_like(slots)
    for h in range(9):
        taken[h] = 0
    for fetch in fetches:
        fetch.wait()
    tile_row, tile_rows = lax.axis_index("gx"), lax.axis_size("gx")
    for b in range(offsets.shape[0]):
        h = heading[b]
        n = taken[h]
        taken[h] = n + 1
        row, col = lax.div(h, 3), lax.rem(h, 3)
        place = col * 9 + row * 3 + n
        slots[place, 0:3, :] = offsets[b]
        slots[place, 3:4, :] = widths[b:b + 1, :]
        slots[place, 4:5, :] = solvation[b:b + 1, :]
        home = tile_row + row - 1
        inside = (home >= 0) & (home < tile_rows)
        slots[place, 5:6, :] = jnp.full((1, 128), jnp.where(inside, 1.0, 0.0), f32)
    even = lax.rem(lax.axis_index("gy"), 2) == 0
    for k, out in ((jnp.where(even, 2, 0), pair_out), (1, same), (jnp.where(even, 0, 2), other_out)):
        out[...] = slots[pl.ds(9 * k, 9)].reshape(out.shape)


def edge_kernel(core, old, first, second, out):
    out[...] = core[...] + old[...]
    even = lax.rem(lax.axis_index("gy"), 2) == 0

    def add(from_left, from_right):
        for i in range(core.shape[0]):
            out[i, 0:5, :] += from_left[i * 5:i * 5 + 5, :]
            out[i, 19:24, :] += from_right[i * 5:i * 5 + 5, :]

    @pl.when(even)
    def _():
        add(second, first)

    @pl.when(jnp.logical_not(even))
    def _():
        add(first, second)


def swapped(value, start):
    pairs = [(k, k + 1) for k in range(start, lax.axis_size("gy") - 1, 2)]
    return lax.ppermute(value, "gy", pairs + [(b, a) for a, b in pairs])


def body(offsets, widths, solvation, heading, old_map):
    depth = old_map.shape[2]
    third = jax.ShapeDtypeStruct((3, 3, 8, 128), f32)
    small = pltpu.CompilerParams(vmem_limit_bytes=8 * 1024 * 1024)
    first, same, second = pl.pallas_call(
        pack_kernel,
        out_shape=[third] * 3,
        in_specs=[HBM] * 4,
        out_specs=[VM] * 3,
        scratch_shapes=[
            pltpu.SMEM((offsets.shape[0],), jnp.int32),
            pltpu.VMEM(offsets.shape, f32),
            pltpu.VMEM(widths.shape, f32),
            pltpu.VMEM(solvation.shape, f32),
            pltpu.VMEM((27, 8, 128), f32),
            pltpu.SMEM((9,), jnp.int32),
            pltpu.SemaphoreType.DMA((4,)),
        ],
        compiler_params=pltpu.CompilerParams(vmem_limit_bytes=60 * 1024 * 1024),
        name="pack",
    )(heading[:, 0], offsets, widths, solvation)
    first, second = swapped(first, 0), swapped(second, 1)
    same, *begun = field("stored", depth, 4, [[(0, 0)], [(0, 1)], [(0, 2)]], [same], keep=True)
    first, second, *begun = lax.optimization_barrier((first, second, *begun))
    own = jnp.concatenate([same, first, second], axis=1)
    count = lax.axis_size("gx")
    partner = lax.ppermute(own, "gx", [(r, r + 1 - 2 * (r % 2)) for r in range(count)])
    even = lax.rem(lax.axis_index("gx"), 2) == 0
    none = jnp.zeros_like(own[0])
    far = jnp.where(
        even,
        jnp.stack([own[2], partner[1], partner[2]]),
        jnp.stack([own[0], partner[1], partner[0]]),
    )
    near = jnp.where(even, own[0:1], own[2:3])
    ahead = [(r, r + 2 - 4 * (r % 2)) for r in range(count)]
    behind = [(r, r - 2 + 4 * (r % 2)) for r in range(count)]
    far = lax.ppermute(far, "gx", [p for p in ahead if 0 <= p[1] < count])
    near = lax.ppermute(near, "gx", [p for p in behind if 0 <= p[1] < count])
    beside = jnp.stack(
        [
            jnp.where(even, none, partner[1]),
            jnp.where(even, partner[0], partner[2]),
            jnp.where(even, partner[1], none),
        ]
    )
    begun = field(
        "chip", depth, 16, [[(0, g), (1, g), (2, g)] for g in range(3)],
        [first, second, beside], begun,
    )
    far, near, *begun = lax.optimization_barrier((far, near, *begun))
    one = jnp.concatenate([near, jnp.zeros_like(near)])
    above, below = jnp.where(even, far[0:2], one), jnp.where(even, one, far[0:2])
    sources, arrays = [[(0, 0), (0, 1)], [(2, 2)], [(1, 0), (1, 1)]], [above, below, far]
    edges = field("rest_edges", depth, 16, sources, arrays, begun[1:], 2)
    first, second = swapped(edges[0], 0), swapped(edges[1], 1)
    (core,) = field("rest_core", depth, 16, sources, arrays, begun[:1], 1)
    core, first, second = lax.optimization_barrier((core, first, second))
    return pl.pallas_call(
        edge_kernel,
        out_shape=jax.ShapeDtypeStruct(old_map.shape, f32),
        in_specs=[VM] * 4,
        out_specs=VM,
        compiler_params=small,
        name="edges",
    )(core.reshape(old_map.shape), old_map, first, second)


def solution(mesh):
    placed = (
        P(("gx", "gy"), None, None),
        P(("gx", "gy"), None),
        P(("gx", "gy"), None),
        P(("gx", "gy"), None),
        P("gx", "gy", None),
    )
    return jax.shard_map(
        body, mesh=mesh, in_specs=placed, out_specs=P("gx", "gy", None), check_vma=False
    )
```

```python
import functools
import jax
import jax.numpy as jnp
from jax import lax
from jax.experimental import pallas as pl
from jax.experimental.pallas import tpu as pltpu
from jax.sharding import PartitionSpec as P

LOG2E = 1.4426950408889634
FAR = 1.0e6
W = 5
f32, bf16 = jnp.float32, jnp.bfloat16
ABOVE, OWN, BELOW = 0, 1, 2
CORE_ROWS = (128, 192, 128)
EDGE_ROWS = (64, 80, 64)


def quotient(n, d):
    return lax.shift_right_logical(n * ((65536 + d - 1) // d), 16)


def put_rows(ti, tj, start, group, core):
    n = (CORE_ROWS if core else EDGE_ROWS)[group]
    if core:
        inner = lax.broadcasted_iota(jnp.int32, (8, 128), 0).astype(f32)
        for v in range(n // 8):
            i, part = divmod(v + (8 if group == BELOW else 0), 3)
            dead = (group == ABOVE and i >= W) or (group == BELOW and i < 8 - W)
            place = FAR if dead else float(i + (8, 0, -8)[group])
            ti[start + v * 8:start + v * 8 + 8, :] = jnp.full((8, 128), place, f32)
            tj[start + v * 8:start + v * 8 + 8, :] = inner + 8.0 * part
        return
    m = lax.broadcasted_iota(jnp.int32, (n, 128), 0)
    side = m >= n // 2
    e = jnp.where(side, m - n // 2, m) + (8 if group == BELOW else 0)
    i = quotient(e, 5)
    right = jnp.logical_xor(side, lax.rem(lax.axis_index("gy"), 2) == 1)
    j = e - i * 5 + jnp.where(right, 24, -W)
    place = (i + (8, 0, -8)[group]).astype(f32)
    if group == ABOVE:
        place = jnp.where(i >= W, FAR, place)
    if group == BELOW:
        place = jnp.where(i < 8 - W, FAR, place)
    ti[start:start + n, :] = place
    tj[start:start + n, :] = j.astype(f32)


def split(v):
    h = v.astype(bf16)
    return h, (v - h.astype(f32)).astype(bf16)


def masks(sources):
    found = []
    for ref, part in sources:
        bits = jnp.zeros((1, 128), f32)
        for s in range(ref.shape[1]):
            bits = bits + ref[part, s, 5:6, :] * float(1 << s)
        found.append(jnp.max(bits).astype(jnp.int32))
    return found


def compact(place, sources, present, shift, count):
    row = lax.broadcasted_iota(jnp.int32, (8, 128), 0)
    for (ref, part), mask in zip(sources, present):
        for s in range(ref.shape[1]):
            place[count] = jnp.where(row == 6, shift, ref[part, s]) if shift else ref[part, s]
            count = count + (lax.shift_right_logical(mask, s) & 1)
    return count


def fill_up(place, count, blocks):
    row = lax.broadcasted_iota(jnp.int32, (8, 128), 0)
    dead = jnp.where(row == 3, 1.0, 0.0).astype(f32)
    for s in range(blocks - 1):
        place[count + s] = dead


def add_field(lists, counts, ti, tj, rows, starts, adds, depth, blocks, wide):
    k_io = lax.broadcasted_iota(jnp.int32, (1, wide), 1).astype(f32)
    dot = functools.partial(jnp.dot, preferred_element_type=f32)

    def stage(g, at, blocks):
        n = rows[g]
        recs = [lists[g, at + q] for q in range(blocks)]
        rec = jnp.concatenate(recs, axis=1)
        x, y, weight = rec[0:1] * 8.0, rec[1:2] * 24.0, rec[4:5]
        c = (-0.5 * LOG2E) / (rec[3:4] * rec[3:4])
        ri, rj = ti[starts[g]:starts[g] + n, :], tj[starts[g]:starts[g] + n, :]
        dx = jnp.concatenate([ri] * blocks, axis=1) - x
        dy = jnp.concatenate([rj] * blocks, axis=1) - y
        ph, plo = split(jnp.exp2((dx * dx + dy * dy) * c) * weight)
        cols = jnp.concatenate([jnp.transpose(r) for r in recs], axis=0)
        z = cols[:, 2:3] * 1024.0
        cz = (-0.5 * LOG2E) / (cols[:, 3:4] * cols[:, 3:4])

        def along(b):
            d = k_io - (z - float(b * wide))
            return split(jnp.exp2(d * (d * cz)))

        nxt = along(0)
        for b in range(depth // wide):
            zh, zl = nxt
            if b + 1 < depth // wide:
                nxt = along(b + 1)
            r = dot(jnp.concatenate([ph, plo, ph], 1), jnp.concatenate([zh, zh, zl], 0))
            for ref, to, count, source in adds[g]:
                ref[to:to + count, b * wide:(b + 1) * wide] += r[source:source + count]

    def together(t, carry):
        for g in range(3):
            stage(g, t * blocks, blocks)
        return carry

    parts = [lax.div(c + blocks // 2, jnp.int32(blocks)) for c in counts]
    joint = jnp.minimum(jnp.minimum(parts[0], parts[1]), parts[2])
    lax.fori_loop(0, joint, together, 0)
    for g in range(3):
        begin = joint * blocks
        left = jnp.maximum(counts[g] - begin, 0)
        whole = lax.div(left + (blocks // 2 - 1), jnp.int32(blocks))

        def step(t, carry, g=g, begin=begin):
            stage(g, begin + t * blocks, blocks)
            return carry

        lax.fori_loop(0, whole, step, 0)

        @pl.when(whole * blocks < left)
        def _(g=g, at=begin + whole * blocks):
            stage(g, at, blocks // 2)


def core_adds(ref):
    return [[(ref, 0, 128, 0)], [(ref, 0, 192, 0)], [(ref, 64, 128, 0)]]


def edge_adds(first, second):
    return [
        [(first, 0, 32, 0), (second, 0, 32, 32)],
        [(first, 0, 40, 0), (second, 0, 40, 40)],
        [(first, 8, 32, 0), (second, 8, 32, 32)],
    ]


def both_adds(core, first, second):
    return [
        a + [(ref, to, n, source + CORE_ROWS[g]) for ref, to, n, source in b]
        for g, (a, b) in enumerate(zip(core_adds(core), edge_adds(first, second)))
    ]


def prepare(ti, tj, kinds):
    rows, starts, at = [], [], 0
    for g in range(3):
        starts.append(at)
        for core in kinds:
            put_rows(ti, tj, at, g, core)
            at += (CORE_ROWS if core else EDGE_ROWS)[g]
        rows.append(at - starts[-1])
    return rows, starts


BLOCKS, WIDE, EDGE_WIDE = 4, 512, 256


def field_kernel(sources, begun, outs, keep, *refs):
    lists, ti, tj = refs[-3:]
    totals, inputs = refs[-3 - outs:-3], refs[:-3 - outs]
    if keep:
        inputs[-1][...] = inputs[0][...]
    depth = totals[0].shape[1]
    rows, starts = prepare(ti, tj, (True, False)[: max(1, outs - 1)])
    for n, ref in enumerate(totals):
        ref[...] = inputs[len(inputs) - outs + n][...] if begun else jnp.zeros_like(ref)
    segments = [[(inputs[n], part) for n, part in sources[g]] for g in range(3)]
    present = [masks(segments[g]) for g in range(3)]
    counts = []
    for g in range(3):
        counts.append(compact(lists.at[g], segments[g], present[g], 0.0, jnp.int32(0)))
        fill_up(lists.at[g], counts[g], BLOCKS)
    adds = both_adds(*totals) if outs == 3 else core_adds(*totals)
    add_field(lists, counts, ti, tj, rows, starts, adds, depth, BLOCKS, WIDE)


def edge_field_kernel(sources, *refs):
    first, second, lists, ti, tj = refs[-5:]
    inputs = refs[:-5]
    depth = first.shape[1]
    put_rows(ti, tj, 0, OWN, False)
    first[...] = inputs[-2][...]
    second[...] = inputs[-1][...]
    segments = [[(inputs[n], part) for n, part in sources[g]] for g in range(3)]
    present = [masks(segments[g]) for g in range(3)]
    count = jnp.int32(0)
    for g in range(3):
        count = compact(lists, segments[g], present[g], (-8.0, 0.0, 8.0)[g], count)
    fill_up(lists, count, 8)
    k_io = lax.broadcasted_iota(jnp.int32, (1, EDGE_WIDE), 1).astype(f32)
    dot = functools.partial(jnp.dot, preferred_element_type=f32)

    def stage(at, blocks):
        recs = [lists[at + q] for q in range(blocks)]
        rec = jnp.concatenate(recs, axis=1)
        x, y, weight = rec[0:1] * 8.0, rec[1:2] * 24.0, rec[4:5]
        c = (-0.5 * LOG2E) / (rec[3:4] * rec[3:4])
        i = jnp.concatenate([ti[...]] * blocks, axis=1) - rec[6:7]
        dx = i - x
        dy = jnp.concatenate([tj[...]] * blocks, axis=1) - y
        value = jnp.exp2((dx * dx + dy * dy) * c) * weight
        ph, plo = split(jnp.where(jnp.abs(i - 3.5) < 4.0 + W, value, 0.0))
        cols = jnp.concatenate([jnp.transpose(r) for r in recs], axis=0)
        z = cols[:, 2:3] * 1024.0
        cz = (-0.5 * LOG2E) / (cols[:, 3:4] * cols[:, 3:4])

        def along(b):
            d = k_io - (z - float(b * EDGE_WIDE))
            return split(jnp.exp2(d * (d * cz)))

        nxt = along(0)
        for b in range(depth // EDGE_WIDE):
            zh, zl = nxt
            if b + 1 < depth // EDGE_WIDE:
                nxt = along(b + 1)
            pp = dot(jnp.concatenate([ph, plo], 0), zh)
            r = pp[:80] + pp[80:] + dot(ph, zl)
            first[:, b * EDGE_WIDE:(b + 1) * EDGE_WIDE] += r[0:40]
            second[:, b * EDGE_WIDE:(b + 1) * EDGE_WIDE] += r[40:80]

    def two(t, carry):
        stage(t * 16, 8)
        stage(t * 16 + 8, 8)
        return carry

    twos = lax.shift_right_logical(count + 1, 4)
    lax.fori_loop(0, twos, two, 0)
    whole = lax.shift_right_logical(count + 1, 3)

    @pl.when(whole > twos * 2)
    def _():
        stage(twos * 16, 8)

    after = count - whole * 8

    @pl.when(after > 2)
    def _():
        stage(whole * 8, 4)

    @pl.when(((after > 0) & (after <= 2)) | (after > 4))
    def _():
        stage(whole * 8 + jnp.where(after > 2, 4, 0), 2)


VM = pl.BlockSpec(memory_space=pltpu.VMEM)
HBM = pl.BlockSpec(memory_space=pltpu.HBM)


def field(name, depth, blocks, sources, arrays, begun=(), outs=3, keep=False):
    operands = (*arrays, *begun)
    shapes = ((192, depth), (40, depth), (40, depth))[:outs]
    rows, place = sum(CORE_ROWS) + sum(EDGE_ROWS), (3, 27 + 2 * BLOCKS, 8, 128)
    kernel = functools.partial(field_kernel, sources, bool(begun), outs, keep)
    if outs == 2:
        shapes, rows, place = ((40, depth),) * 2, EDGE_ROWS[OWN], (81 + 8, 8, 128)
        kernel = functools.partial(edge_field_kernel, sources)
    if keep:
        shapes = (arrays[0].shape, *shapes)
    return pl.pallas_call(
        kernel,
        out_shape=[jax.ShapeDtypeStruct(s, f32) for s in shapes],
        in_specs=[VM] * len(operands),
        out_specs=[VM] * len(shapes),
        scratch_shapes=[
            pltpu.VMEM(place, f32),
            pltpu.VMEM((rows, 128), f32),
            pltpu.VMEM((rows, 128), f32),
        ],
        compiler_params=pltpu.CompilerParams(vmem_limit_bytes=32 * 1024 * 1024),
        cost_estimate=pl.CostEstimate(
            flops=blocks * 200_000_000, bytes_accessed=4_000_000, transcendentals=blocks * 300_000
        ),
        name=name,
    )(*operands)


def pack_kernel(*refs):
    hbm, (pair_out, same, other_out), local, (slots, taken, sems) = refs[:4], refs[4:7], refs[7:11], refs[11:]
    fetches = [pltpu.make_async_copy(a, b, sems.at[n]) for n, (a, b) in enumerate(zip(hbm, local))]
    for fetch in fetches:
        fetch.start()
    heading, offsets, widths, solvation = local
    slots[...] = jnp.zeros_like(slots)
    for h in range(9):
        taken[h] = 0
    for fetch in fetches:
        fetch.wait()
    tile_row, tile_rows = lax.axis_index("gx"), lax.axis_size("gx")
    for b in range(offsets.shape[0]):
        h = heading[b]
        n = taken[h]
        taken[h] = n + 1
        row, col = lax.div(h, 3), lax.rem(h, 3)
        place = col * 9 + row * 3 + n
        slots[place, 0:3, :] = offsets[b]
        slots[place, 3:4, :] = widths[b:b + 1, :]
        slots[place, 4:5, :] = solvation[b:b + 1, :]
        home = tile_row + row - 1
        inside = (home >= 0) & (home < tile_rows)
        slots[place, 5:6, :] = jnp.full((1, 128), jnp.where(inside, 1.0, 0.0), f32)
    even = lax.rem(lax.axis_index("gy"), 2) == 0
    for k, out in ((jnp.where(even, 2, 0), pair_out), (1, same), (jnp.where(even, 0, 2), other_out)):
        out[...] = slots[pl.ds(9 * k, 9)].reshape(out.shape)


def edge_kernel(core, old, first, second, out):
    out[...] = core[...] + old[...]
    even = lax.rem(lax.axis_index("gy"), 2) == 0

    def add(from_left, from_right):
        for i in range(core.shape[0]):
            out[i, 0:5, :] += from_left[i * 5:i * 5 + 5, :]
            out[i, 19:24, :] += from_right[i * 5:i * 5 + 5, :]

    @pl.when(even)
    def _():
        add(first, second)

    @pl.when(jnp.logical_not(even))
    def _():
        add(second, first)


def swapped(value, start):
    pairs = [(k, k + 1) for k in range(start, lax.axis_size("gy") - 1, 2)]
    return lax.ppermute(value, "gy", pairs + [(b, a) for a, b in pairs])


def body(offsets, widths, solvation, heading, old_map):
    depth = old_map.shape[2]
    third = jax.ShapeDtypeStruct((3, 3, 8, 128), f32)
    small = pltpu.CompilerParams(vmem_limit_bytes=8 * 1024 * 1024)
    first, same, second = pl.pallas_call(
        pack_kernel,
        out_shape=[third] * 3,
        in_specs=[HBM] * 4,
        out_specs=[VM] * 3,
        scratch_shapes=[
            pltpu.SMEM((offsets.shape[0],), jnp.int32),
            pltpu.VMEM(offsets.shape, f32),
            pltpu.VMEM(widths.shape, f32),
            pltpu.VMEM(solvation.shape, f32),
            pltpu.VMEM((27, 8, 128), f32),
            pltpu.SMEM((9,), jnp.int32),
            pltpu.SemaphoreType.DMA((4,)),
        ],
        compiler_params=pltpu.CompilerParams(vmem_limit_bytes=60 * 1024 * 1024),
        name="pack",
    )(heading[:, 0], offsets, widths, solvation)
    first, second = swapped(first, 0), swapped(second, 1)
    same, *begun = field("stored", depth, 4, [[(0, 0)], [(0, 1)], [(0, 2)]], [same], keep=True)
    first, second, *begun = lax.optimization_barrier((first, second, *begun))
    own = jnp.concatenate([same, first, second], axis=1)
    count = lax.axis_size("gx")
    partner = lax.ppermute(own, "gx", [(r, r + 1 - 2 * (r % 2)) for r in range(count)])
    even = lax.rem(lax.axis_index("gx"), 2) == 0
    none = jnp.zeros_like(own[0])
    far = jnp.where(
        even,
        jnp.stack([own[2], partner[1], partner[2]]),
        jnp.stack([own[0], partner[1], partner[0]]),
    )
    near = jnp.where(even, own[0:1], own[2:3])
    ahead = [(r, r + 2 - 4 * (r % 2)) for r in range(count)]
    behind = [(r, r - 2 + 4 * (r % 2)) for r in range(count)]
    far = lax.ppermute(far, "gx", [p for p in ahead if 0 <= p[1] < count])
    near = lax.ppermute(near, "gx", [p for p in behind if 0 <= p[1] < count])
    beside = jnp.stack(
        [
            jnp.where(even, none, partner[1]),
            jnp.where(even, partner[0], partner[2]),
            jnp.where(even, partner[1], none),
        ]
    )
    begun = field(
        "chip", depth, 16, [[(0, g), (1, g), (2, g)] for g in range(3)],
        [first, second, beside], begun,
    )
    far, near, *begun = lax.optimization_barrier((far, near, *begun))
    one = jnp.concatenate([near, jnp.zeros_like(near)])
    above, below = jnp.where(even, far[0:2], one), jnp.where(even, one, far[0:2])
    sources, arrays = [[(0, 0), (0, 1)], [(2, 2)], [(1, 0), (1, 1)]], [above, below, far]
    edges = field("rest_edges", depth, 16, sources, arrays, begun[1:], 2)
    first, second = swapped(edges[0], 1), swapped(edges[1], 0)
    (core,) = field("rest_core", depth, 16, sources, arrays, begun[:1], 1)
    core, first, second = lax.optimization_barrier((core, first, second))
    return pl.pallas_call(
        edge_kernel,
        out_shape=jax.ShapeDtypeStruct(old_map.shape, f32),
        in_specs=[VM] * 4,
        out_specs=VM,
        compiler_params=small,
        name="edges",
    )(core.reshape(old_map.shape), old_map, first, second)


def solution(mesh):
    placed = (
        P(("gx", "gy"), None, None),
        P(("gx", "gy"), None),
        P(("gx", "gy"), None),
        P(("gx", "gy"), None),
        P("gx", "gy", None),
    )
    return jax.shard_map(
        body, mesh=mesh, in_specs=placed, out_specs=P("gx", "gy", None), check_vma=False
    )
```
